32 devices in a mesh: shots: 2 (over y), depth: 4 (over z), row: 4 (over x, core).
Axes of the slice: x: 2, y: 2, z: 4, core: 2. Of those that a mesh axis runs over, the one named last changes fastest.
Arguments:
- waves: float32 [8, 2, 512, 2, 1, 512], P(('shots', 'depth'), None, 'row'), parts along dimension 0, may hold values from -6 to 6
- slab_freq: float32 [8, 1], P(('shots', 'depth')), parts along dimension 0, may hold values from 1.2 to 2.4
- slowness: float32 [4, 512, 512], P('depth', 'row'), may hold values from 0.8 to 1.25
- ref_slow: float32 [4], P('depth'), may hold values from 0.9 to 1.1
- inj_freq: float32 [2, 1], P('shots'), parts along dimension 0, may hold values from 1.2 to 2.4
- wavelet: float32 [2, 1, 2], P('shots'), parts along dimension 0, may hold values from -64 to 64
- records: float32 [2, 1, 2, 4096], P('shots'), parts along dimension 0, may hold values from -6 to 6
- src_pos: int32 [4], P('shots'), parts along dimension 0, may hold values from 0 to 511
- rcv_pos: int32 [8192, 2], P('shots'), parts along dimension 0, may hold values from 0 to 511
Outputs:
- wave_out: float32 [8, 2, 512, 2, 1, 512], P(('shots', 'depth'), None, 'row'), parts along dimension 0
- image: float32 [8, 16, 512, 512], P(('shots', 'depth'), None, 'row'), parts along dimension 0
The draws below stay inside these ranges and needn't reach their ends.
There are 2 independent parts, one for each index of `shots`. The reference program is written for one: setup_inputs(seed, part) draws one part's arguments, and reference() takes and returns one part's arrays. A program takes and returns all parts, laid end to end along the dimension named above; an argument that names none is the same for every part. Nothing has to cross between parts.
All inputs are finite; a program needn't handle non-finite values.
Results may differ from the reference program's by a relative error of at most 0.0003.
Values sent between devices are 32-bit elements; how exact they have to be, the bound alone decides.
No kernel may reach another device: no remote copies, remote signals or barrier semaphores. Data moves between devices by JAX's collectives and lax.ppermute only.
A program may use at most 128 MiB of HBM per device.

```python
import math
import jax
import jax.numpy as jnp
from jax import lax

NL = 512
OFF = 16
F = 1
PLANES_DEV = 1
TICKS = 2
NREC = 4096
DZ = 4
GROUPS = 4
DEPTHS = 4


def place_ends(entries, key, smallest, top_value):
    extent = entries.shape
    spot = [jax.random.randint(jax.random.fold_in(key, axis), (), 0, extent[axis]) for axis in range(len(extent))]
    entries = entries.at[tuple(spot)].set(smallest)
    longest = extent.index(max(extent))
    spot[longest] = (spot[longest] + 1) % extent[longest]
    return entries.at[tuple(spot)].set(top_value)


def block_levels(rng, extent, split, least, largest):
    factor_of = 1.0
    for position, shards_of in split:
        steps = jax.random.uniform(jax.random.fold_in(jax.random.fold_in(rng, 6), position), (shards_of,), jnp.float32, least / len(split), largest / len(split))
        factor_of = factor_of * jnp.repeat(jnp.exp(steps), extent[position] // shards_of).reshape((-1,) + (1,) * (len(extent) - 1 - position))
    return factor_of


def scatter_about(stream_key, shape, width, most, pieces=(), kind=jnp.bfloat16):
    values = width * jax.random.normal(stream_key, shape, jnp.float32)
    if pieces:
        values = values * block_levels(stream_key, shape, pieces, -0.22, 0.18)
    return jnp.clip(values, -most, most).astype(kind)


def setup_inputs(seed: int = 0, part: int = 0) -> dict:
    seeds = jax.random.split(jax.random.key(seed), 10)
    own_keys = jax.random.split(jax.random.fold_in(seeds[9], part), 10)
    return {
        "waves": scatter_about(own_keys[0], (GROUPS, 2, NL, 2, F, NL), 1.0, 6.0, ((0, 4), (2, 4)), jnp.float32),
        "slab_freq": jnp.clip(1.2 + 1.2 * jax.random.uniform(own_keys[1], (GROUPS, F), jnp.float32) ** block_levels(own_keys[1], (GROUPS, F), ((0, 4),), -0.2, 0.2), 1.2, 2.4),
        "slowness": jnp.clip(jnp.exp(math.log(1.25) - 0.4462871 * jax.random.uniform(seeds[2], (DEPTHS, NL, NL), jnp.float32) ** block_levels(seeds[2], (DEPTHS, NL, NL), ((0, 4), (1, 4)), -0.2, 0.2)), 0.8, 1.25),
        "ref_slow": jnp.clip(0.9 + 0.20000005 * jax.random.uniform(seeds[3], (DEPTHS,), jnp.float32) ** block_levels(seeds[3], (DEPTHS,), ((0, 4),), -0.2, 0.2), 0.9, 1.1),
        "inj_freq": jnp.clip(jax.random.uniform(own_keys[4], (TICKS - 1, F), jnp.float32, 1.2, 2.4), 1.2, 2.4),
        "wavelet": scatter_about(own_keys[5], (TICKS - 1, F, 2), 16.0, 64.0, (), jnp.float32),
        "records": scatter_about(own_keys[6], (TICKS - 1, F, 2, NREC), 1.0, 6.0, (), jnp.float32),
        "src_pos": jax.random.randint(own_keys[7], (2,), 0, NL).astype(jnp.int32),
        "rcv_pos": place_ends(jax.random.randint(own_keys[8], (NREC, 2), 0, NL), jax.random.fold_in(own_keys[8], 1), 0, NL - 1).astype(jnp.int32),
    }


def inject(tick_now, wavelet, records, src_pos, rcv_pos):
    lateral_cells = jnp.arange(NL, dtype=jnp.int32)
    source_point = ((lateral_cells == src_pos[0])[:, None] & (lateral_cells == src_pos[1])[None, :]).astype(jnp.float32)
    amplitude = wavelet[tick_now, :, 0] + 1j * wavelet[tick_now, :, 1]
    source = amplitude[:, None, None] * source_point[None]
    recorded = records[tick_now, :, 0] + 1j * records[tick_now, :, 1]
    receiver = jnp.zeros((F, NL, NL), recorded.dtype).at[:, rcv_pos[:, 0], rcv_pos[:, 1]].add(recorded)
    return jnp.stack([source, receiver])

def reference(waves, slab_freq, slowness, ref_slow, inj_freq, wavelet, records, src_pos, rcv_pos):
    half_width = OFF // 2
    wave_field = waves[:, 0] + 1j * waves[:, 1]
    wave_field = jnp.transpose(wave_field, (0, 2, 3, 1, 4))
    field_signs = jnp.array([1.0, -1.0], jnp.float32)[None, :, None, None, None]
    wave_numbers = jnp.fft.fftfreq(NL) * (2.0 * math.pi)
    wave_sq = wave_numbers[:, None] ** 2 + wave_numbers[None, :] ** 2
    freq_now = slab_freq
    slow_planes = slowness.reshape(GROUPS, PLANES_DEV, NL, NL)
    ref_planes = ref_slow.reshape(GROUPS, PLANES_DEV)
    image_sum = jnp.zeros((GROUPS, PLANES_DEV, OFF, NL, NL), jnp.float32)
    for tick_now in range(TICKS):
        for plane_index in range(PLANES_DEV):
            ref_number = freq_now * ref_planes[:, plane_index][:, None]
            vertical_sq = (ref_number * ref_number)[:, :, None, None] - wave_sq
            root_abs = jnp.sqrt(jnp.abs(vertical_sq))
            propagating = vertical_sq > 0
            phase_real = jnp.where(propagating, jnp.cos(root_abs * DZ), jnp.exp(-root_abs * DZ))
            phase_imag = jnp.where(propagating, jnp.sin(root_abs * DZ), 0.0)
            phase_shift = phase_real[:, None] + 1j * field_signs * phase_imag[:, None]
            wave_field = jnp.fft.ifft2(jnp.fft.fft2(wave_field) * phase_shift)
            contrast = slow_planes[:, plane_index] - ref_planes[:, plane_index][:, None, None]
            lens_angle = field_signs * freq_now[:, None, :, None, None] * contrast[:, None, None] * DZ
            wave_field = wave_field * (jnp.cos(lens_angle) + 1j * jnp.sin(lens_angle))
            padded = jnp.pad(wave_field, ((0, 0), (0, 0), (0, 0), (half_width, half_width), (0, 0)))
            offset_terms = []
            for offset_index in range(OFF):
                offset_lag = offset_index - half_width
                source = padded[:, 0, :, half_width - offset_lag:half_width - offset_lag + NL]
                receiver = padded[:, 1, :, half_width + offset_lag:half_width + offset_lag + NL]
                product = jnp.real(source) * jnp.real(receiver) + jnp.imag(source) * jnp.imag(receiver)
                offset_terms.append(lax.optimization_barrier(jnp.sum(product, axis=1)))
            image_sum = image_sum.at[:, plane_index].add(jnp.stack(offset_terms, axis=1))
        if tick_now + 1 < TICKS:
            injected = inject(tick_now, wavelet, records, src_pos, rcv_pos)
            wave_field = jnp.concatenate([injected[None], wave_field[:-1]], axis=0)
            freq_now = jnp.concatenate([inj_freq[tick_now][None], freq_now[:-1]], axis=0)
    wave_field = jnp.transpose(wave_field, (0, 3, 1, 2, 4))
    wave_out = jnp.stack([jnp.real(wave_field), jnp.imag(wave_field)], axis=1).astype(jnp.float32)
    image = image_sum.reshape(GROUPS * PLANES_DEV, OFF, NL, NL).astype(jnp.float32)
    return (wave_out, image)
```

```python
import functools
import math

import jax
import jax.numpy as jnp
import ml_dtypes
import numpy as np
from jax import lax
from jax.experimental import pallas as pl
from jax.experimental.pallas import tpu as pltpu
from jax.sharding import PartitionSpec as P

OFF = 16
HALF = OFF // 2
DZ = 4
LANES = 128
MIB = 1024 * 1024

F32 = jnp.float32
BF16 = jnp.bfloat16


def wave_order(length):
    place = np.arange(length)
    half = length // 2
    return np.where(place < half, 2 * place, 2 * (place - half) + 1)


def two_parts(table):
    high = table.astype(ml_dtypes.bfloat16)
    low = (table - high.astype(np.float64)).astype(ml_dtypes.bfloat16)
    return np.stack([high, low])


@functools.lru_cache(maxsize=None)
def tables(length, slices):
    half, cols = length // 2, length // slices
    product = wave_order(length)[:, None] * np.arange(half)[None, :] % length
    angle = product * (2.0 * math.pi / length)
    pair = np.stack([np.cos(angle), np.sin(angle)])
    by_parity = pair.reshape(2, 2, half, half)
    x_forward = by_parity.transpose(1, 0, 2, 3).reshape(2, 2 * half, half)
    x_inverse = by_parity.transpose(1, 0, 3, 2).reshape(2, 2 * half, half)
    y_inverse = pair.reshape(2, slices, cols, half)
    y_forward = y_inverse.transpose(0, 1, 3, 2)
    return tuple(two_parts(t) for t in (x_forward, x_inverse, y_forward, y_inverse))


def parts_of(value):
    high = value.astype(BF16)
    return high, (value - high.astype(F32)).astype(BF16)


def dot(a, b):
    return jnp.dot(a, b, preferred_element_type=F32)


def sin_cos(angle):
    turns = jnp.floor(angle * (2.0 / math.pi) + 0.5)
    rest = angle - turns * 1.5703125
    rest = rest - turns * 4.837512969970703125e-4
    rest = rest - turns * 7.54978995489188216e-8
    square = rest * rest
    sine = rest + rest * square * (
        -1.6666654611e-1 + square * (8.3321608736e-3 - square * 1.9515295891e-4)
    )
    cosine = 1.0 + square * (
        -0.5
        + square * (4.166664568298827e-2 + square * (-1.388731625493765e-3 + square * 2.443315711809948e-5))
    )
    quarter = turns.astype(jnp.int32)
    swap = (quarter & 1) == 1
    sine_out = jnp.where(swap, cosine, sine)
    cosine_out = jnp.where(swap, sine, cosine)
    sine_out = jnp.where((quarter & 2) == 2, -sine_out, sine_out)
    cosine_out = jnp.where(((quarter + 1) & 2) == 2, -cosine_out, cosine_out)
    return sine_out, cosine_out


def along_y(real, imag, table, index, inverse):
    rows = real.shape[0]
    real_high, real_low = parts_of(real)
    imag_high, imag_low = parts_of(imag)
    stacked = jnp.concatenate([real_high, imag_high, real_low, imag_low], axis=0)
    products = []
    for which in range(2):
        both = dot(stacked, table[0, which, index])
        products.append(
            both[: 2 * rows] + (both[2 * rows :] + dot(stacked[: 2 * rows], table[1, which, index]))
        )
    cosines, sines = products
    if inverse:
        return cosines[:rows] - sines[rows:], cosines[rows:] + sines[:rows]
    return cosines[:rows] + sines[rows:], cosines[rows:] - sines[:rows]


def along_x(real, imag, table, parity, inverse):
    half = real.shape[0]
    products = []
    for value in (real, imag):
        high, low = parts_of(value)
        products.append(
            dot(table[0, parity], high)
            + (dot(table[0, parity], low) + dot(table[1, parity], high))
        )
    by_real, by_imag = products
    if inverse:
        return by_real[:half] - by_imag[half:], by_imag[:half] + by_real[half:]
    return by_real[:half] + by_imag[half:], by_imag[:half] - by_real[half:]


class Layout:
    def __init__(self, ranks, groups, rows, lateral):
        self.ranks, self.groups, self.rows, self.lateral = ranks, groups, rows, lateral
        self.slices = ranks // 2
        self.half = lateral // 2
        self.cols = lateral // self.slices
        self.chunks = lateral // LANES

    def place(self):
        rank = lax.axis_index("row")
        return rank % self.slices, rank // self.slices


def first_kernel(lay, *refs):
    waves, y_forward = refs[:2]
    pieces = refs[2 : 2 + lay.ranks]
    parity_parts = refs[-1]
    index, side = lay.place()
    middle = lay.chunks // 2
    for field in range(2):
        for part in range(2):
            chunks = [
                waves[
                    pl.ds(
                        (part * lay.rows * 2 + field) * lay.chunks + chunk,
                        lay.rows,
                        stride=2 * lay.chunks,
                    ),
                    :,
                ]
                for chunk in range(lay.chunks)
            ]
            low = jnp.concatenate(chunks[:middle], axis=1)
            high = jnp.concatenate(chunks[middle:], axis=1)
            parity_parts[2 * field, part] = low + high
            parity_parts[2 * field + 1, part] = low - high
    for step in reversed(range(lay.ranks)):
        piece_slice = index ^ (step % lay.slices)
        field = side ^ (step // lay.slices)
        at = 2 * field + piece_slice // (lay.slices // 2)
        real, imag = along_y(
            parity_parts[at, 0], parity_parts[at, 1], y_forward, piece_slice, False
        )
        pieces[step][0] = real
        pieces[step][1] = imag


def column_kernel(lay, first, *refs):
    count_in = lay.ranks if first else lay.slices
    count_out = lay.slices if first else lay.ranks
    pieces = refs[:count_in]
    phase, x_forward, x_inverse = refs[count_in : count_in + 3]
    results = refs[count_in + 3 : count_in + 3 + count_out]
    parity_parts, halves = refs[-2:]
    index, side = lay.place()
    sign = (1 - 2 * side).astype(F32)
    for step in range(lay.slices):
        at = pl.ds(pl.multiple_of((index ^ step) * lay.rows, lay.rows), lay.rows)
        for part in range(2):
            if first:
                low, high = pieces[step][part], pieces[step + lay.slices][part]
                difference = (low - high) * sign
            else:
                low, high = pieces[step][0, part], pieces[step][1, part]
                difference = low - high
            parity_parts[0, part, at, :] = low + high
            parity_parts[1, part, at, :] = difference
    sums = []
    for parity in range(2):
        real, imag = along_x(
            parity_parts[parity, 0], parity_parts[parity, 1], x_forward, parity, False
        )
        phase_real, phase_imag = phase[0, parity], phase[1, parity]
        sums.append(
            along_x(
                real * phase_real - imag * phase_imag,
                real * phase_imag + imag * phase_real,
                x_inverse,
                parity,
                True,
            )
        )
    for part in range(2):
        halves[0, part] = sums[0][part] + sums[1][part]
        halves[1, part] = sums[0][part] - sums[1][part]
    for step in range(count_out):
        block = (index ^ (step % lay.slices)) * lay.rows
        at = pl.ds(pl.multiple_of(block, lay.rows), lay.rows)
        for part in range(2):
            if first:
                for upper in range(2):
                    results[step][upper, part] = halves[upper, part, at, :]
            else:
                results[step][part] = halves[side ^ (step // lay.slices), part, at, :]


def rows_from(lay, pieces, y_inverse, index):
    low, high = None, None
    for step, (real, imag) in enumerate(pieces):
        piece_slice = index ^ step
        sign = (1 - 2 * (piece_slice // (lay.slices // 2))).astype(F32)
        part = along_y(real, imag, y_inverse, piece_slice, True)
        turned = [value * sign for value in part]
        low = part if low is None else [a + b for a, b in zip(low, part)]
        high = turned if high is None else [a + b for a, b in zip(high, turned)]
    return low, high


def middle_kernel(lay, *refs):
    pieces = refs[: lay.slices]
    lens, injected, y_inverse, y_forward = refs[lay.slices : lay.slices + 4]
    own, other = refs[lay.slices + 4 : lay.slices + 6]
    results = refs[lay.slices + 6 : 2 * lay.slices + 6]
    fields, parity_parts = refs[-2:]
    index, side = lay.place()
    last = lax.axis_index("depth") == lay.groups - 1
    both = 2 * lay.rows
    low, high = rows_from(
        lay,
        [[piece[:, part].reshape(both, lay.cols) for part in range(2)] for piece in pieces],
        y_inverse,
        index,
    )
    for end, (real, imag) in enumerate((low, high)):
        lanes = pl.ds(end * lay.half, lay.half)
        cosine = lens[0, :, :, lanes].reshape(both, lay.half)
        sine = lens[1, :, :, lanes].reshape(both, lay.half)
        shape = (2, lay.rows, lay.half)
        fields[:, 0, :, lanes] = (real * cosine - imag * sine).reshape(shape)
        fields[:, 1, :, lanes] = (real * sine + imag * cosine).reshape(shape)
    for part in range(2):
        own[part] = fields[side, part]
        other[part] = fields[1 - side, part]
    for part in range(2):
        ends = []
        for end in range(2):
            lanes = pl.ds(end * lay.half, lay.half)
            value = jnp.where(last, injected[part, :, :, lanes], fields[:, part, :, lanes])
            ends.append(value.reshape(both, lay.half))
        parity_parts[0, part] = ends[0] + ends[1]
        parity_parts[1, part] = ends[0] - ends[1]
    for step in range(lay.slices):
        piece_slice = index ^ step
        at = piece_slice // (lay.slices // 2)
        pair = along_y(parity_parts[at, 0], parity_parts[at, 1], y_forward, piece_slice, False)
        for part in range(2):
            results[step][:, part] = pair[part].reshape(2, lay.rows, lay.cols)


def last_kernel(lay, *refs):
    pieces = refs[: lay.ranks]
    lens, y_inverse = refs[lay.ranks : lay.ranks + 2]
    wave_out, own, other, leading, trailing = refs[lay.ranks + 2 : lay.ranks + 7]
    fields = refs[-1]
    index, side = lay.place()
    for turn, result in enumerate((own, other)):
        field = side ^ turn
        low, high = rows_from(
            lay,
            [
                [piece[0], piece[1]]
                for piece in pieces[turn * lay.slices : (turn + 1) * lay.slices]
            ],
            y_inverse,
            index,
        )
        sign = (1 - 2 * field).astype(F32)
        for end, (real, imag) in enumerate((low, high)):
            lanes = pl.ds(end * lay.half, lay.half)
            cosine, sine = lens[0, :, lanes], lens[1, :, lanes] * sign
            result[0, :, lanes] = real * cosine - imag * sine
            result[1, :, lanes] = real * sine + imag * cosine
        for part in range(2):
            fields[field, part] = result[part]
            leading[turn, part] = result[part, :HALF]
            trailing[turn, part] = result[part, lay.rows - HALF :]
    for field in range(2):
        for part in range(2):
            for chunk in range(lay.chunks):
                start = (part * lay.rows * 2 + field) * lay.chunks + chunk
                wave_out[pl.ds(start, lay.rows, stride=2 * lay.chunks), :] = fields[
                    field, part, :, pl.ds(chunk * LANES, LANES)
                ]


def image_kernel(lay, adds, *refs):
    own, other, before, after = refs[:4]
    result, padded = refs[-2:]
    rank = lax.axis_index("row")
    side = rank // lay.slices
    side_before = (rank + lay.ranks - 1) % lay.ranks // lay.slices
    side_after = (rank + 1) % lay.ranks // lay.slices
    end = HALF + lay.rows
    for part in range(2):
        padded[side, part, HALF:end] = own[part]
        padded[1 - side, part, HALF:end] = other[part]
        for field in range(2):
            padded[field, part, :HALF] = before[field ^ side_before, part]
            padded[field, part, end:] = after[field ^ side_after, part]
    for offset in range(OFF):
        lag = offset - HALF
        source = pl.ds(HALF - lag, lay.rows)
        receiver = pl.ds(HALF + lag, lay.rows)
        value = (
            padded[0, 0, source] * padded[1, 0, receiver]
            + padded[0, 1, source] * padded[1, 1, receiver]
        )
        result[offset] = refs[4][offset] + value if adds else value


def prepare_kernel(lay, freq, freq_injected, ref_own, ref_next, source_at, wavelet, records, receivers, phase_a, phase_b, injected, sums):
    index, side = lay.place()
    last = lax.axis_index("depth") == lay.groups - 1
    shape = (lay.half, lay.cols)
    spacing = 2.0 * math.pi / lay.lateral

    def squares(even_odd):
        signed = jnp.where(even_odd < lay.half, even_odd, even_odd - lay.lateral)
        number = signed.astype(F32) * spacing
        return number * number

    place = lax.broadcasted_iota(jnp.int32, shape, 1) + index * lay.cols
    y_squares = squares(jnp.where(place < lay.half, 2 * place, 2 * (place - lay.half) + 1))
    scale = 1.0 / (lay.lateral * lay.lateral)
    sign = (1 - 2 * side).astype(F32) * scale
    wave_numbers = (
        freq[0, 0] * ref_own[0],
        jnp.where(last, freq_injected[0, 0], freq[0, 0]) * ref_next[0],
    )
    for parity in range(2):
        x_squares = squares(2 * lax.broadcasted_iota(jnp.int32, shape, 0) + parity)
        lateral_squares = x_squares + y_squares
        for number, phase in zip(wave_numbers, (phase_a, phase_b)):
            vertical = number * number - lateral_squares
            argument = jnp.sqrt(jnp.abs(vertical)) * DZ
            sine, cosine = sin_cos(argument)
            runs = vertical > 0
            phase[0, parity] = jnp.where(runs, cosine, jnp.exp(-argument)) * scale
            phase[1, parity] = jnp.where(runs, sine, 0.0) * sign

    count = receivers.shape[1]
    width = next((w for w in (1024, 512, 256, 128) if count % w == 0), count)
    both = 2 * lay.rows
    is_source = side == 0
    row = lax.broadcasted_iota(jnp.int32, (both, width), 0)
    row = row + index * lay.rows + jnp.where(row >= lay.rows, (lay.slices - 1) * lay.rows, 0)
    column = lax.broadcasted_iota(jnp.int32, (lay.lateral, width), 0)
    for start in range(0, count, width):
        lanes = pl.ds(start, width)
        is_first = lax.broadcasted_iota(jnp.int32, (1, width), 1) + start == 0
        at_row = jnp.where(
            is_source, jnp.where(is_first, source_at[0], -1), receivers[0:1, lanes]
        )
        at_column = jnp.where(is_source, source_at[1], receivers[1:2, lanes])
        hit = row == at_row
        stacked = []
        for part in range(2):
            value = jnp.where(is_source, wavelet[0, part], records[part : part + 1, lanes])
            high = value.astype(BF16).astype(F32)
            for piece in (high, value - high):
                stacked.append(jnp.where(hit, piece, 0.0).astype(BF16))
        picked = jnp.where(column == at_column, 1.0, 0.0).astype(BF16)
        found = lax.dot_general(
            jnp.concatenate(stacked, axis=0),
            picked,
            (((1,), (1,)), ((), ())),
            preferred_element_type=F32,
        )
        sums[...] = found if start == 0 else sums[...] + found
    for part in range(2):
        at = 2 * part * both
        value = sums[at : at + both] + sums[at + both : at + 2 * both]
        injected[part] = value.reshape(2, lay.rows, lay.lateral)


def lens_kernel(lay, freq, ref_own, slow_own, slow_other, lens):
    index, side = lay.place()
    sign = (1 - 2 * side).astype(F32)
    for turn, slow in enumerate((slow_own, slow_other)):
        at = side ^ turn
        sine, cosine = sin_cos(sign * freq[0, 0] * (slow[...] - ref_own[0]) * DZ)
        lens[0, at] = cosine
        lens[1, at] = sine


def last_lens_kernel(lay, freq_before, freq_injected, ref_own, slow, lens):
    top = lax.axis_index("depth") == 0
    freq = jnp.where(top, freq_injected[0, 0], freq_before[0, 0])
    sine, cosine = sin_cos(freq * (slow[...] - ref_own[0]) * DZ)
    lens[0] = cosine
    lens[1] = sine


def call(kernel, outs, scratch, args, scalars=(), flops=0, nbytes=0, name=None):
    vmem = pl.BlockSpec(memory_space=pltpu.VMEM)
    smem = pl.BlockSpec(memory_space=pltpu.SMEM)
    shapes = [jax.ShapeDtypeStruct(shape, F32) for shape in outs]
    return pl.pallas_call(
        kernel,
        out_shape=shapes,
        in_specs=[smem if i in scalars else vmem for i in range(len(args))],
        out_specs=[vmem] * len(outs),
        scratch_shapes=[pltpu.VMEM(shape, F32) for shape in scratch],
        compiler_params=pltpu.CompilerParams(vmem_limit_bytes=40 * MIB),
        cost_estimate=pl.CostEstimate(
            flops=int(flops), bytes_accessed=int(nbytes), transcendentals=0
        ),
        name=name,
    )(*args)


def local(waves, slab_freq, slowness, ref_slow, inj_freq, wavelet, records, src_pos, rcv_pos):
    ranks, groups = lax.axis_size("row"), lax.axis_size("depth")
    rows, lateral = waves.shape[2], waves.shape[5]
    lay = Layout(ranks, groups, rows, lateral)
    slices, cols, half = lay.slices, lay.cols, lay.half
    x_forward, x_inverse, y_forward, y_inverse = (
        jnp.asarray(table) for table in tables(lateral, slices)
    )
    slow = slowness[0]

    def exchange(value, step):
        return lax.ppermute(value, "row", [(rank, rank ^ step) for rank in range(ranks)])

    def onward(value, step):
        pairs = [
            (group * ranks + rank, (group + 1) % groups * ranks + (rank ^ step))
            for group in range(groups)
            for rank in range(ranks)
        ]
        return lax.ppermute(value, ("depth", "row"), pairs)

    piece = (2, rows, cols)
    pair_piece = (2, 2, rows, cols)
    block = (2, rows, lateral)
    edge = (2, 2, HALF, lateral)
    flat = (2 * rows * 2 * lay.chunks, LANES)

    sent = call(
        functools.partial(first_kernel, lay),
        [piece] * ranks,
        [(4, 2, rows, half)],
        [waves.reshape(flat), y_forward],
        name="rows_to_columns",
    )
    arrived = [sent[0]] + [None] * (ranks - 1)
    for step in reversed(range(1, ranks)):
        arrived[step] = exchange(sent[step], step)

    freq_before = lax.ppermute(slab_freq, "depth", [(i, i + 1) for i in range(groups - 1)])
    ref_next = lax.ppermute(ref_slow, "depth", [(i, (i - 1) % groups) for i in range(groups)])
    phase = (2, 2, half, cols)
    phase_a, phase_b, injected = call(
        functools.partial(prepare_kernel, lay),
        [phase, phase, (2, 2, rows, lateral)],
        [(8 * rows, lateral)],
        [
            slab_freq,
            inj_freq,
            ref_slow,
            ref_next,
            src_pos,
            wavelet[0],
            records.reshape(2, -1),
            rcv_pos.T,
        ],
        scalars=(0, 1, 2, 3, 4, 5),
        flops=4e9,
        name="phases_and_injection",
    )
    (last_lens,) = call(
        functools.partial(last_lens_kernel, lay),
        [block],
        [],
        [freq_before, inj_freq, ref_slow, slow],
        scalars=(0, 1, 2),
        name="last_lens",
    )
    slow_sent, arrived = lax.optimization_barrier((slow, arrived))
    slow_other = exchange(slow_sent, slices)

    sent = call(
        functools.partial(column_kernel, lay, True),
        [pair_piece] * slices,
        [(2, 2, half, cols)] * 2,
        [*arrived, phase_a, x_forward, x_inverse],
        name="columns_first",
    )
    arrived = [sent[0]] + [exchange(sent[step], step) for step in range(1, slices)]
    (lens,) = call(
        functools.partial(lens_kernel, lay),
        [(2, 2, rows, lateral)],
        [],
        [slab_freq, ref_slow, slow, slow_other],
        scalars=(0, 1),
        name="lens",
    )
    own, other, *sent = call(
        functools.partial(middle_kernel, lay),
        [block, block] + [pair_piece] * slices,
        [(2, 2, rows, lateral), (2, 2, 2 * rows, half)],
        [*arrived, lens, injected, y_inverse, y_forward],
        name="columns_to_columns",
    )
    arrived = [sent[0]] + [exchange(sent[step], step) for step in range(1, slices)]
    other = exchange(other, slices)

    sent = call(
        functools.partial(column_kernel, lay, False),
        [piece] * ranks,
        [(2, 2, half, cols)] * 2,
        [*arrived, phase_b, x_forward, x_inverse],
        name="columns_second",
    )
    arrived = [None] * ranks
    for step in reversed(range(ranks)):
        arrived[step] = onward(sent[step], step)

    up = [(rank, rank + 1) for rank in range(ranks - 1)]
    down = [(rank + 1, rank) for rank in range(ranks - 1)]

    def image(own, other, leading, trailing, previous):
        before = lax.ppermute(trailing, "row", up)
        after = lax.ppermute(leading, "row", down)
        args = [own, other, before, after]
        if previous is not None:
            args.append(previous)
        (result,) = call(
            functools.partial(image_kernel, lay, previous is not None),
            [(OFF, rows, lateral)],
            [(2, 2, rows + OFF, lateral)],
            args,
            name="image",
        )
        return result

    previous = image(
        own,
        other,
        jnp.stack([own[:, :HALF], other[:, :HALF]]),
        jnp.stack([own[:, rows - HALF :], other[:, rows - HALF :]]),
        None,
    )
    wave_out, own, other, leading, trailing = call(
        functools.partial(last_kernel, lay),
        [flat, block, block, edge, edge],
        [(2, 2, rows, lateral)],
        [*arrived, last_lens, y_inverse],
        name="columns_to_rows",
    )
    result = image(own, other, leading, trailing, previous)
    return wave_out.reshape(waves.shape), result[None]


def solution(mesh):
    placed = (
        P(("shots", "depth"), None, "row", None, None, None),
        P(("shots", "depth"), None),
        P("depth", "row", None),
        P("depth"),
        P("shots", None),
        P("shots", None, None),
        P("shots", None, None, None),
        P("shots"),
        P("shots", None),
    )
    return jax.shard_map(
        local,
        mesh=mesh,
        in_specs=placed,
        out_specs=(
            P(("shots", "depth"), None, "row", None, None, None),
            P(("shots", "depth"), None, "row", None),
        ),
        check_vma=False,
    )
```

```python
import functools
import math

import jax
import jax.numpy as jnp
import ml_dtypes
import numpy as np
from jax import lax
from jax.experimental import pallas as pl
from jax.experimental.pallas import tpu as pltpu
from jax.sharding import PartitionSpec as P

OFF = 16
HALF = OFF // 2
DZ = 4
LANES = 128
MIB = 1024 * 1024

F32 = jnp.float32
BF16 = jnp.bfloat16


def wave_order(length):
    place = np.arange(length)
    half = length // 2
    return np.where(place < half, 2 * place, 2 * (place - half) + 1)


def two_parts(table):
    high = table.astype(ml_dtypes.bfloat16)
    low = (table - high.astype(np.float64)).astype(ml_dtypes.bfloat16)
    return np.stack([high, low])


@functools.lru_cache(maxsize=None)
def tables(length, slices):
    half, cols = length // 2, length // slices
    product = wave_order(length)[:, None] * np.arange(half)[None, :] % length
    angle = product * (2.0 * math.pi / length)
    pair = np.stack([np.cos(angle), np.sin(angle)])
    by_parity = pair.reshape(2, 2, half, half)
    x_forward = by_parity.transpose(1, 0, 2, 3).reshape(2, 2 * half, half)
    x_inverse = by_parity.transpose(1, 0, 3, 2).reshape(2, 2 * half, half)
    y_inverse = pair.reshape(2, slices, cols, half)
    y_forward = y_inverse.transpose(0, 1, 3, 2)
    return tuple(two_parts(t) for t in (x_forward, x_inverse, y_forward, y_inverse))


def parts_of(value):
    high = value.astype(BF16)
    return high, (value - high.astype(F32)).astype(BF16)


def dot(a, b):
    return jnp.dot(a, b, preferred_element_type=F32)


def sin_cos(angle):
    turns = jnp.floor(angle * (2.0 / math.pi) + 0.5)
    rest = angle - turns * 1.5703125
    rest = rest - turns * 4.837512969970703125e-4
    rest = rest - turns * 7.54978995489188216e-8
    square = rest * rest
    sine = rest + rest * square * (
        -1.6666654611e-1 + square * (8.3321608736e-3 - square * 1.9515295891e-4)
    )
    cosine = 1.0 + square * (
        -0.5
        + square * (4.166664568298827e-2 + square * (-1.388731625493765e-3 + square * 2.443315711809948e-5))
    )
    quarter = turns.astype(jnp.int32)
    swap = (quarter & 1) == 1
    sine_out = jnp.where(swap, cosine, sine)
    cosine_out = jnp.where(swap, sine, cosine)
    sine_out = jnp.where((quarter & 2) == 2, -sine_out, sine_out)
    cosine_out = jnp.where(((quarter + 1) & 2) == 2, -cosine_out, cosine_out)
    return sine_out, cosine_out


def along_y(real, imag, table, index, inverse):
    rows = real.shape[0]
    real_high, real_low = parts_of(real)
    imag_high, imag_low = parts_of(imag)
    stacked = jnp.concatenate([real_high, imag_high, real_low, imag_low], axis=0)
    products = []
    for which in range(2):
        both = dot(stacked, table[0, which, index])
        products.append(
            both[: 2 * rows] + (both[2 * rows :] + dot(stacked[: 2 * rows], table[1, which, index]))
        )
    cosines, sines = products
    if inverse:
        return cosines[:rows] - sines[rows:], cosines[rows:] + sines[:rows]
    return cosines[:rows] + sines[rows:], cosines[rows:] - sines[:rows]


def along_x(real, imag, table, parity, inverse):
    half = real.shape[0]
    products = []
    for value in (real, imag):
        high, low = parts_of(value)
        products.append(
            dot(table[0, parity], high)
            + (dot(table[0, parity], low) + dot(table[1, parity], high))
        )
    by_real, by_imag = products
    if inverse:
        return by_real[:half] - by_imag[half:], by_imag[:half] + by_real[half:]
    return by_real[:half] + by_imag[half:], by_imag[:half] - by_real[half:]


class Layout:
    def __init__(self, ranks, groups, rows, lateral):
        self.ranks, self.groups, self.rows, self.lateral = ranks, groups, rows, lateral
        self.slices = ranks // 2
        self.half = lateral // 2
        self.cols = lateral // self.slices
        self.chunks = lateral // LANES
        self.wide = rows + OFF

    def place(self):
        rank = lax.axis_index("row")
        return rank % self.slices, rank // self.slices


def first_kernel(lay, *refs):
    far, pieces = refs[:2], refs[2 : 2 + lay.ranks]
    parity_parts, waves, y_forward, arrivals = refs[2 + lay.ranks :]
    index, side = lay.place()
    middle = lay.chunks // 2
    copies = [
        pltpu.make_async_copy(source, target, arrivals.at[i])
        for i, (source, target) in enumerate(zip(far, (waves, y_forward)))
    ]
    for copy in copies:
        copy.start()
    copies[0].wait()
    for field in range(2):
        for part in range(2):
            chunks = [
                waves[
                    pl.ds(
                        (part * lay.rows * 2 + field) * lay.chunks + chunk,
                        lay.rows,
                        stride=2 * lay.chunks,
                    ),
                    :,
                ]
                for chunk in range(lay.chunks)
            ]
            low = jnp.concatenate(chunks[:middle], axis=1)
            high = jnp.concatenate(chunks[middle:], axis=1)
            parity_parts[2 * field, part] = low + high
            parity_parts[2 * field + 1, part] = low - high
    copies[1].wait()
    for step in reversed(range(lay.ranks)):
        piece_slice = index ^ (step % lay.slices)
        field = side ^ (step // lay.slices)
        at = 2 * field + piece_slice // (lay.slices // 2)
        real, imag = along_y(
            parity_parts[at, 0], parity_parts[at, 1], y_forward, piece_slice, False
        )
        pieces[step][0] = real
        pieces[step][1] = imag


def column_kernel(lay, first, *refs):
    count_in = lay.ranks if first else lay.slices
    count_out = lay.slices if first else lay.ranks
    pieces = refs[:count_in]
    phase, x_forward, x_inverse_far = refs[count_in : count_in + 3]
    results = refs[-4 - count_out : -4]
    parity_parts, whole, x_inverse, x_inverse_here = refs[-4:]
    x_inverse_copy = pltpu.make_async_copy(x_inverse_far, x_inverse, x_inverse_here)
    x_inverse_copy.start()
    index, side = lay.place()
    sign = (1 - 2 * side).astype(F32)
    for step in range(lay.slices):
        at = pl.ds(pl.multiple_of((index ^ step) * lay.rows, lay.rows), lay.rows)
        for part in range(2):
            if first:
                low, high = pieces[step][part], pieces[step + lay.slices][part]
                difference = (low - high) * sign
            else:
                low, high = pieces[step][0, part], pieces[step][1, part]
                difference = low - high
            parity_parts[0, part, at, :] = low + high
            parity_parts[1, part, at, :] = difference
    sums = []
    for parity in range(2):
        real, imag = along_x(
            parity_parts[parity, 0], parity_parts[parity, 1], x_forward, parity, False
        )
        phase_real, phase_imag = phase[0, parity], phase[1, parity]
        if parity == 0:
            x_inverse_copy.wait()
        sums.append(
            along_x(
                real * phase_real - imag * phase_imag,
                real * phase_imag + imag * phase_real,
                x_inverse,
                parity,
                True,
            )
        )
    for part in range(2):
        whole[part, :HALF] = jnp.zeros((HALF, lay.cols), F32)
        whole[part, HALF : HALF + lay.half] = sums[0][part] + sums[1][part]
        whole[part, HALF + lay.half : HALF + lay.lateral] = sums[0][part] - sums[1][part]
        whole[part, HALF + lay.lateral :] = jnp.zeros((HALF, lay.cols), F32)
    if first:
        for step in range(lay.slices):
            for upper in range(2):
                place = ((index ^ step) + upper * lay.slices) * lay.rows
                at = pl.ds(pl.multiple_of(place + HALF, 8), lay.rows)
                for part in range(2):
                    results[step][upper, part] = whole[part, at, :]
        return
    results[0][0, lay.wide :] = refs[count_in + 3][...]
    for step in range(lay.ranks):
        place = ((index + side * lay.slices) ^ step) * lay.rows
        at = pl.ds(pl.multiple_of(place, 8), lay.wide)
        for part in range(2):
            results[step][part, : lay.wide] = whole[part, at, :]


def rows_from(lay, pieces, y_inverse, index):
    low, high = None, None
    for step, (real, imag) in enumerate(pieces):
        piece_slice = index ^ step
        sign = (1 - 2 * (piece_slice // (lay.slices // 2))).astype(F32)
        part = along_y(real, imag, y_inverse, piece_slice, True)
        turned = [value * sign for value in part]
        low = part if low is None else [a + b for a, b in zip(low, part)]
        high = turned if high is None else [a + b for a, b in zip(high, turned)]
    return low, high


def middle_kernel(lay, *refs):
    pieces = refs[: lay.slices]
    lens, injected, y_inverse, y_forward = refs[lay.slices : lay.slices + 4]
    own, other = refs[lay.slices + 4 : lay.slices + 6]
    results = refs[lay.slices + 6 : 2 * lay.slices + 6]
    fields, parity_parts = refs[-2:]
    index, side = lay.place()
    last = lax.axis_index("depth") == lay.groups - 1
    both = 2 * lay.rows
    low, high = rows_from(
        lay,
        [[piece[:, part].reshape(both, lay.cols) for part in range(2)] for piece in pieces],
        y_inverse,
        index,
    )
    for end, (real, imag) in enumerate((low, high)):
        lanes = pl.ds(end * lay.half, lay.half)
        cosine = lens[0, :, :, lanes].reshape(both, lay.half)
        sine = lens[1, :, :, lanes].reshape(both, lay.half)
        shape = (2, lay.rows, lay.half)
        fields[:, 0, :, lanes] = (real * cosine - imag * sine).reshape(shape)
        fields[:, 1, :, lanes] = (real * sine + imag * cosine).reshape(shape)
    for part in range(2):
        own[part] = fields[side, part]
        other[part] = fields[1 - side, part]
    for part in range(2):
        ends = []
        for end in range(2):
            lanes = pl.ds(end * lay.half, lay.half)
            value = jnp.where(last, injected[part, :, :, lanes], fields[:, part, :, lanes])
            ends.append(value.reshape(both, lay.half))
        parity_parts[0, part] = ends[0] + ends[1]
        parity_parts[1, part] = ends[0] - ends[1]
    for step in range(lay.slices):
        piece_slice = index ^ step
        at = piece_slice // (lay.slices // 2)
        pair = along_y(parity_parts[at, 0], parity_parts[at, 1], y_forward, piece_slice, False)
        for part in range(2):
            results[step][:, part] = pair[part].reshape(2, lay.rows, lay.cols)


def last_kernel(lay, *refs):
    pieces = refs[: lay.ranks]
    slow, ref_own, before, behind, y_inverse, previous = refs[lay.ranks : lay.ranks + 6]
    wave_out, image = refs[lay.ranks + 6 : lay.ranks + 8]
    lens, fields, wave_buffer, image_buffer, wave_sent, image_sent = refs[lay.ranks + 8 :]
    index, side = lay.place()
    freq = pieces[0][0, lay.wide : lay.wide + 1, 0:1]
    end = HALF + lay.rows
    for start, values in ((0, before[4]), (HALF, slow[...]), (end, behind[4])):
        sine, cosine = sin_cos(freq * (values - ref_own[0]) * DZ)
        lens[0, start : start + values.shape[0]] = cosine
        lens[1, start : start + values.shape[0]] = sine
    for turn in range(2):
        field = side ^ turn
        sign = (1 - 2 * field).astype(F32)
        ends = rows_from(
            lay,
            [
                [piece[part, : lay.wide] for part in range(2)]
                for piece in pieces[turn * lay.slices : (turn + 1) * lay.slices]
            ],
            y_inverse,
            index,
        )
        for end, (real, imag) in enumerate(ends):
            lanes = pl.ds(end * lay.half, lay.half)
            cosine, sine = lens[0, :, lanes], lens[1, :, lanes] * sign
            fields[field, 0, :, lanes] = real * cosine - imag * sine
            fields[field, 1, :, lanes] = real * sine + imag * cosine
    for field in range(2):
        for part in range(2):
            for chunk in range(lay.chunks):
                start = (part * lay.rows * 2 + field) * lay.chunks + chunk
                wave_buffer[pl.ds(start, lay.rows, stride=2 * lay.chunks), :] = fields[
                    field, part, HALF : HALF + lay.rows, pl.ds(chunk * LANES, LANES)
                ]
    copies = [pltpu.make_async_copy(wave_buffer, wave_out, wave_sent)]
    copies[0].start()
    for offset in range(OFF):
        image_buffer[offset] = previous[offset] + correlation(lay, fields, offset)
        copies.append(
            pltpu.make_async_copy(
                image_buffer.at[offset], image.at[offset], image_sent.at[offset]
            )
        )
        copies[-1].start()
    for copy in copies:
        copy.wait()


def correlation(lay, fields, offset):
    lag = offset - HALF
    source = pl.ds(HALF - lag, lay.rows)
    receiver = pl.ds(HALF + lag, lay.rows)
    return (
        fields[0, 0, source] * fields[1, 0, receiver]
        + fields[0, 1, source] * fields[1, 1, receiver]
    )


def image_kernel(lay, own, other, before, after, result, fields):
    rank = lax.axis_index("row")
    side = rank // lay.slices
    side_before = (rank + lay.ranks - 1) % lay.ranks // lay.slices
    side_after = (rank + 1) % lay.ranks // lay.slices
    end = HALF + lay.rows
    for part in range(2):
        fields[side, part, HALF:end] = own[part]
        fields[1 - side, part, HALF:end] = other[part]
        for field in range(2):
            fields[field, part, :HALF] = before[2 * (field ^ side_before) + part]
            fields[field, part, end:] = after[2 * (field ^ side_after) + part]
    for offset in range(OFF):
        result[offset] = correlation(lay, fields, offset)


def fill_phase(lay, wave_number, phase):
    index, side = lay.place()
    shape = (lay.half, lay.cols)
    spacing = 2.0 * math.pi / lay.lateral

    def squares(even_odd):
        signed = jnp.where(even_odd < lay.half, even_odd, even_odd - lay.lateral)
        number = signed.astype(F32) * spacing
        return number * number

    place = lax.broadcasted_iota(jnp.int32, (1, lay.cols), 1) + index * lay.cols
    y_squares = squares(jnp.where(place < lay.half, 2 * place, 2 * (place - lay.half) + 1))
    scale = 1.0 / (lay.lateral * lay.lateral)
    sign = (1 - 2 * side).astype(F32) * scale
    for parity in range(2):
        x_squares = squares(2 * lax.broadcasted_iota(jnp.int32, shape, 0) + parity)
        vertical = wave_number * wave_number - (x_squares + y_squares)
        argument = jnp.sqrt(jnp.abs(vertical)) * DZ
        sine, cosine = sin_cos(argument)
        runs = vertical > 0
        phase[0, parity] = jnp.where(runs, cosine, jnp.exp(-argument)) * scale
        phase[1, parity] = jnp.where(runs, sine, 0.0) * sign


def phase_kernel(lay, freq, ref_own, phase):
    fill_phase(lay, freq[0, 0] * ref_own[0], phase)


def next_phase_kernel(lay, freq, freq_injected, ref_next, phase, freq_rows):
    last = lax.axis_index("depth") == lay.groups - 1
    freq_now = jnp.where(last, freq_injected[0, 0], freq[0, 0])
    fill_phase(lay, freq_now * ref_next[0], phase)
    freq_rows[...] = jnp.zeros((8, lay.cols), F32) + freq_now


def inject_kernel(lay, *refs):
    far, injected = refs[:4], refs[4]
    sums, near, arrivals = refs[5], refs[6:10], refs[10]
    copies = [
        pltpu.make_async_copy(source, target, arrivals.at[i])
        for i, (source, target) in enumerate(zip(far, near))
    ]
    for copy in copies:
        copy.start()
    index, side = lay.place()
    source_at, wavelet, records, receivers = near
    count = receivers.shape[1]
    width = next((w for w in (1024, 512, 256, 128) if count % w == 0), count)
    both = 2 * lay.rows
    is_source = side == 0
    row = lax.broadcasted_iota(jnp.int32, (both, width), 0)
    row = row + index * lay.rows + jnp.where(row >= lay.rows, (lay.slices - 1) * lay.rows, 0)
    column = lax.broadcasted_iota(jnp.int32, (lay.lateral, width), 0)
    for copy in copies:
        copy.wait()
    for start in range(0, count, width):
        lanes = pl.ds(start, width)
        is_first = lax.broadcasted_iota(jnp.int32, (1, width), 1) + start == 0
        at_row = jnp.where(
            is_source, jnp.where(is_first, source_at[:, 0:1], -1), receivers[0:1, lanes]
        )
        at_column = jnp.where(is_source, source_at[:, 1:2], receivers[1:2, lanes])
        hit = row == at_row
        stacked = []
        for part in range(2):
            value = jnp.where(
                is_source, wavelet[:, part : part + 1], records[part : part + 1, lanes]
            )
            high = value.astype(BF16).astype(F32)
            for piece in (high, value - high):
                stacked.append(jnp.where(hit, piece, 0.0).astype(BF16))
        picked = jnp.where(column == at_column, 1.0, 0.0).astype(BF16)
        found = lax.dot_general(
            jnp.concatenate(stacked, axis=0),
            picked,
            (((1,), (1,)), ((), ())),
            preferred_element_type=F32,
        )
        sums[...] = found if start == 0 else sums[...] + found
    for part in range(2):
        at = 2 * part * both
        value = sums[at : at + both] + sums[at + both : at + 2 * both]
        injected[part] = value.reshape(2, lay.rows, lay.lateral)


def lens_kernel(lay, freq, ref_own, slow, *refs):
    lens = refs[-1]
    _, side = lay.place()
    sign = (1 - 2 * side).astype(F32)

    def store(field, start, values):
        sine, cosine = sin_cos(sign * freq[0, 0] * (values - ref_own[0]) * DZ)
        at = pl.ds(pl.multiple_of(start, 8), values.shape[0])
        lens[0, field, at, :] = cosine
        lens[1, field, at, :] = sine

    store(side, 0, slow[...])
    shot = lax.axis_index("shots")
    for step, part in enumerate(refs[:-1]):
        start = (shot ^ step) * part.shape[0] if len(refs) > 2 else 0
        store(1 - side, start, part[...])


def after(*values):
    return lax.optimization_barrier(values)


def call(kernel, outs, scratch, args, scalars=(), far=(), outside=False, vmem=40, name=None):
    inside = pl.BlockSpec(memory_space=pltpu.VMEM)
    smem = pl.BlockSpec(memory_space=pltpu.SMEM)
    outer = pl.BlockSpec(memory_space=pltpu.HBM)
    anywhere = pl.BlockSpec(memory_space=pl.ANY)
    shapes = [jax.ShapeDtypeStruct(shape, F32) for shape in outs]
    args = [
        pltpu.with_memory_space_constraint(value, pltpu.HBM) if i in far else value
        for i, value in enumerate(args)
    ]
    return pl.pallas_call(
        kernel,
        out_shape=shapes,
        in_specs=[
            smem if i in scalars else outer if i in far else inside for i in range(len(args))
        ],
        out_specs=[anywhere if outside else inside] * len(outs),
        scratch_shapes=[
            pltpu.VMEM(shape, F32) if isinstance(shape, tuple) else shape for shape in scratch
        ],
        compiler_params=pltpu.CompilerParams(vmem_limit_bytes=vmem * MIB),
        cost_estimate=pl.CostEstimate(
            flops=1, bytes_accessed=1, transcendentals=0
        ),
        name=name,
    )(*args)


def local(waves, slab_freq, slowness, ref_slow, inj_freq, wavelet, records, src_pos, rcv_pos):
    ranks, groups = lax.axis_size("row"), lax.axis_size("depth")
    rows, lateral = waves.shape[2], waves.shape[5]
    lay = Layout(ranks, groups, rows, lateral)
    slices, cols, half = lay.slices, lay.cols, lay.half
    x_forward, x_inverse, y_forward, y_inverse = (
        jnp.asarray(table) for table in tables(lateral, slices)
    )
    slow = slowness[0]

    def exchange(value, step):
        return lax.ppermute(value, "row", [(rank, rank ^ step) for rank in range(ranks)])

    def onward(value, step):
        pairs = [
            (group * ranks + rank, (group + 1) % groups * ranks + (rank ^ step))
            for group in range(groups)
            for rank in range(ranks)
        ]
        return lax.ppermute(value, ("depth", "row"), pairs)

    piece = (2, rows, cols)
    pair_piece = (2, 2, rows, cols)
    block = (2, rows, lateral)
    wide = lay.wide
    flat = (2 * rows * 2 * lay.chunks, LANES)

    shots = lax.axis_size("shots")
    if shots & (shots - 1) or rows % (8 * shots):
        shots = 1
    share = rows // shots
    shot = lax.axis_index("shots") if shots > 1 else 0
    slow_parts = [exchange(lax.dynamic_slice_in_dim(slow, shot * share, share), slices)]

    phase = (2, 2, half, cols)
    column_scratch = [
        (2, 2, half, cols),
        (2, lateral + OFF, cols),
        pltpu.VMEM(x_inverse.shape, BF16),
        pltpu.SemaphoreType.DMA(()),
    ]
    sent = call(
        functools.partial(first_kernel, lay),
        [piece] * ranks,
        [
            (4, 2, rows, half),
            flat,
            pltpu.VMEM(y_forward.shape, BF16),
            pltpu.SemaphoreType.DMA((2,)),
        ],
        [waves.reshape(flat), y_forward],
        far=(0, 1),
        name="rows_to_columns",
    )
    sent, slow_parts = after(sent, slow_parts)
    arrived = [sent[0]] + [None] * (ranks - 1)
    for step in reversed(range(1, ranks)):
        arrived[step] = exchange(sent[step], step)
    for step in range(1, shots):
        pairs = [(shot, shot ^ step) for shot in range(shots)]
        slow_parts.append(lax.ppermute(slow_parts[0], "shots", pairs))

    ref_sent, _ = after(ref_slow, sent[1])
    ref_next = lax.ppermute(ref_sent, "depth", [(i, (i - 1) % groups) for i in range(groups)])
    (phase_a,) = call(
        functools.partial(phase_kernel, lay),
        [phase],
        [],
        [slab_freq, ref_slow],
        scalars=(0, 1),
        name="phase_first",
    )
    receivers = [src_pos[None], wavelet[0], records.reshape(2, -1), rcv_pos.T]
    receivers[0], ref_next = after(receivers[0], ref_next)
    (injected,) = call(
        functools.partial(inject_kernel, lay),
        [(2, 2, rows, lateral)],
        [(8 * rows, lateral)]
        + [pltpu.VMEM(value.shape, value.dtype) for value in receivers]
        + [pltpu.SemaphoreType.DMA((4,))],
        receivers,
        far=(0, 1, 2, 3),
        name="injection",
    )
    phase_a, slow_parts, injected = after(phase_a, slow_parts, injected)
    sent = call(
        functools.partial(column_kernel, lay, True),
        [pair_piece] * slices,
        column_scratch,
        [*arrived, phase_a, x_forward, x_inverse],
        far=(ranks + 2,),
        name="columns_first",
    )
    freq_now, sent = after(slab_freq, sent)
    arrived = [sent[0]] + [exchange(sent[step], step) for step in range(1, slices)]
    (lens,) = call(
        functools.partial(lens_kernel, lay),
        [(2, 2, rows, lateral)],
        [],
        [freq_now, ref_slow, slow, *slow_parts],
        scalars=(0, 1),
        name="lens",
    )
    own, other, *sent = call(
        functools.partial(middle_kernel, lay),
        [block, block] + [pair_piece] * slices,
        [(2, 2, rows, lateral), (2, 2, 2 * rows, half)],
        [*arrived, lens, injected, y_inverse, y_forward],
        name="columns_to_columns",
    )
    arrived = [sent[0]] + [exchange(sent[step], step) for step in range(1, slices)]
    other = exchange(other, slices)
    phase_b, freq_rows = call(
        functools.partial(next_phase_kernel, lay),
        [phase, (8, cols)],
        [],
        [slab_freq, inj_freq, ref_next],
        scalars=(0, 1, 2),
        name="phase_second",
    )

    sent = call(
        functools.partial(column_kernel, lay, False),
        [(2, wide + 8, cols)] + [(2, wide, cols)] * (ranks - 1),
        column_scratch,
        [*arrived, phase_b, x_forward, x_inverse, freq_rows],
        far=(slices + 2,),
        name="columns_second",
    )
    arrived = [onward(value, step) for step, value in enumerate(sent)]

    def beside(rows_at, pairs):
        planes = [own[0], own[1], other[0], other[1], slow]
        return lax.ppermute(jnp.stack([plane[rows_at] for plane in planes]), "row", pairs)

    before = beside(slice(rows - HALF, rows), [(rank, rank + 1) for rank in range(ranks - 1)])
    behind = beside(slice(0, HALF), [(rank + 1, rank) for rank in range(ranks - 1)])
    (previous,) = call(
        functools.partial(image_kernel, lay),
        [(OFF, rows, lateral)],
        [(2, 2, wide, lateral)],
        [own, other, before, behind],
        name="image_first",
    )
    wave_out, result = call(
        functools.partial(last_kernel, lay),
        [flat, (OFF, rows, lateral)],
        [
            (2, wide, lateral),
            (2, 2, wide, lateral),
            flat,
            (OFF, rows, lateral),
            pltpu.SemaphoreType.DMA(()),
            pltpu.SemaphoreType.DMA((OFF,)),
        ],
        [*arrived, slow, ref_slow, before, behind, y_inverse, previous],
        scalars=(ranks + 1,),
        outside=True,
        name="last_rows_and_image",
    )
    return wave_out.reshape(waves.shape), result[None]


def solution(mesh):
    placed = (
        P(("shots", "depth"), None, "row", None, None, None),
        P(("shots", "depth"), None),
        P("depth", "row", None),
        P("depth"),
        P("shots", None),
        P("shots", None, None),
        P("shots", None, None, None),
        P("shots"),
        P("shots", None),
    )
    return jax.shard_map(
        local,
        mesh=mesh,
        in_specs=placed,
        out_specs=(
            P(("shots", "depth"), None, "row", None, None, None),
            P(("shots", "depth"), None, "row", None),
        ),
        check_vma=False,
    )
```

```python
import functools
import math

import jax
import jax.numpy as jnp
import ml_dtypes
import numpy as np
from jax import lax
from jax.experimental import pallas as pl
from jax.experimental.pallas import tpu as pltpu
from jax.sharding import PartitionSpec as P

OFF = 16
HALF = OFF // 2
DZ = 4
LANES = 128
MIB = 1024 * 1024

F32 = jnp.float32
BF16 = jnp.bfloat16


def wave_order(length):
    place = np.arange(length)
    half = length // 2
    return np.where(place < half, 2 * place, 2 * (place - half) + 1)


def two_parts(table):
    high = table.astype(ml_dtypes.bfloat16)
    low = (table - high.astype(np.float64)).astype(ml_dtypes.bfloat16)
    return np.stack([high, low])


@functools.lru_cache(maxsize=None)
def tables(length, slices):
    half, cols = length // 2, length // slices
    product = wave_order(length)[:, None] * np.arange(half)[None, :] % length
    angle = product * (2.0 * math.pi / length)
    pair = np.stack([np.cos(angle), np.sin(angle)])
    by_parity = pair.reshape(2, 2, half, half)
    x_forward = by_parity.transpose(1, 0, 2, 3).reshape(2, 2 * half, half)
    x_inverse = by_parity.transpose(1, 0, 3, 2).reshape(2, 2 * half, half)
    y_inverse = pair.reshape(2, slices, cols, half)
    y_forward = y_inverse.transpose(0, 1, 3, 2)
    return tuple(two_parts(t) for t in (x_forward, x_inverse, y_forward, y_inverse))


def parts_of(value):
    high = value.astype(BF16)
    return high, (value - high.astype(F32)).astype(BF16)


def dot(a, b):
    return jnp.dot(a, b, preferred_element_type=F32)


def sin_cos(angle):
    turns = jnp.floor(angle * (2.0 / math.pi) + 0.5)
    rest = angle - turns * 1.5703125
    rest = rest - turns * 4.837512969970703125e-4
    rest = rest - turns * 7.54978995489188216e-8
    square = rest * rest
    sine = rest + rest * square * (
        -1.6666654611e-1 + square * (8.3321608736e-3 - square * 1.9515295891e-4)
    )
    cosine = 1.0 + square * (
        -0.5
        + square * (4.166664568298827e-2 + square * (-1.388731625493765e-3 + square * 2.443315711809948e-5))
    )
    quarter = turns.astype(jnp.int32)
    swap = (quarter & 1) == 1
    sine_out = jnp.where(swap, cosine, sine)
    cosine_out = jnp.where(swap, sine, cosine)
    sine_out = jnp.where((quarter & 2) == 2, -sine_out, sine_out)
    cosine_out = jnp.where(((quarter + 1) & 2) == 2, -cosine_out, cosine_out)
    return sine_out, cosine_out


def along_y(real, imag, table, index, inverse):
    rows = real.shape[0]
    real_high, real_low = parts_of(real)
    imag_high, imag_low = parts_of(imag)
    stacked = jnp.concatenate([real_high, imag_high, real_low, imag_low], axis=0)
    products = []
    for which in range(2):
        both = dot(stacked, table[0, which, index])
        products.append(
            both[: 2 * rows] + (both[2 * rows :] + dot(stacked[: 2 * rows], table[1, which, index]))
        )
    cosines, sines = products
    if inverse:
        return cosines[:rows] - sines[rows:], cosines[rows:] + sines[:rows]
    return cosines[:rows] + sines[rows:], cosines[rows:] - sines[:rows]


def along_x(real, imag, table, parity, inverse):
    half = real.shape[0]
    products = []
    for value in (real, imag):
        high, low = parts_of(value)
        products.append(
            dot(table[0, parity], high)
            + (dot(table[0, parity], low) + dot(table[1, parity], high))
        )
    by_real, by_imag = products
    if inverse:
        return by_real[:half] - by_imag[half:], by_imag[:half] + by_real[half:]
    return by_real[:half] + by_imag[half:], by_imag[:half] - by_real[half:]


class Layout:
    def __init__(self, ranks, groups, rows, lateral):
        self.ranks, self.groups, self.rows, self.lateral = ranks, groups, rows, lateral
        self.slices = ranks // 2
        self.half = lateral // 2
        self.cols = lateral // self.slices
        self.chunks = lateral // LANES
        self.wide = rows + OFF

    def place(self):
        rank = lax.axis_index("row")
        return rank % self.slices, rank // self.slices


def first_kernel(lay, *refs):
    far, pieces = refs[:2], refs[2 : 2 + lay.ranks]
    parity_parts, waves, y_forward, arrivals = refs[2 + lay.ranks :]
    index, side = lay.place()
    middle = lay.chunks // 2
    copies = [
        pltpu.make_async_copy(source, target, arrivals.at[i])
        for i, (source, target) in enumerate(zip(far, (waves, y_forward)))
    ]
    for copy in copies:
        copy.start()
    copies[0].wait()
    for field in range(2):
        for part in range(2):
            chunks = [
                waves[
                    pl.ds(
                        (part * lay.rows * 2 + field) * lay.chunks + chunk,
                        lay.rows,
                        stride=2 * lay.chunks,
                    ),
                    :,
                ]
                for chunk in range(lay.chunks)
            ]
            low = jnp.concatenate(chunks[:middle], axis=1)
            high = jnp.concatenate(chunks[middle:], axis=1)
            parity_parts[2 * field, part] = low + high
            parity_parts[2 * field + 1, part] = low - high
    copies[1].wait()
    for step in reversed(range(lay.ranks)):
        piece_slice = index ^ (step % lay.slices)
        field = side ^ (step // lay.slices)
        at = 2 * field + piece_slice // (lay.slices // 2)
        real, imag = along_y(
            parity_parts[at, 0], parity_parts[at, 1], y_forward, piece_slice, False
        )
        pieces[step][0] = real
        pieces[step][1] = imag


def column_kernel(lay, first, *refs):
    count_in = lay.ranks if first else lay.slices
    count_out = lay.slices if first else lay.ranks
    pieces = refs[:count_in]
    phase, x_forward, x_inverse_far = refs[count_in : count_in + 3]
    results = refs[-4 - count_out : -4]
    parity_parts, whole, x_inverse, x_inverse_here = refs[-4:]
    x_inverse_copy = pltpu.make_async_copy(x_inverse_far, x_inverse, x_inverse_here)
    x_inverse_copy.start()
    index, side = lay.place()
    sign = (1 - 2 * side).astype(F32)
    for step in range(lay.slices):
        at = pl.ds(pl.multiple_of((index ^ step) * lay.rows, lay.rows), lay.rows)
        for part in range(2):
            if first:
                low, high = pieces[step][part], pieces[step + lay.slices][part]
                difference = (low - high) * sign
            else:
                low, high = pieces[step][0, part], pieces[step][1, part]
                difference = low - high
            parity_parts[0, part, at, :] = low + high
            parity_parts[1, part, at, :] = difference
    shifted = []
    for parity in range(2):
        real, imag = along_x(
            parity_parts[parity, 0], parity_parts[parity, 1], x_forward, parity, False
        )
        phase_real, phase_imag = phase[0, parity], phase[1, parity]
        shifted.append(
            (real * phase_real - imag * phase_imag, real * phase_imag + imag * phase_real)
        )
    x_inverse_copy.wait()
    sums = [along_x(*shifted[parity], x_inverse, parity, True) for parity in range(2)]
    for part in range(2):
        whole[part, :HALF] = jnp.zeros((HALF, lay.cols), F32)
        whole[part, HALF : HALF + lay.half] = sums[0][part] + sums[1][part]
        whole[part, HALF + lay.half : HALF + lay.lateral] = sums[0][part] - sums[1][part]
        whole[part, HALF + lay.lateral :] = jnp.zeros((HALF, lay.cols), F32)
    if first:
        for step in range(lay.slices):
            for upper in range(2):
                place = ((index ^ step) + upper * lay.slices) * lay.rows
                at = pl.ds(pl.multiple_of(place + HALF, 8), lay.rows)
                for part in range(2):
                    results[step][upper, part] = whole[part, at, :]
        return
    results[0][0, lay.wide :] = refs[count_in + 3][...]
    for step in range(lay.ranks):
        place = ((index + side * lay.slices) ^ step) * lay.rows
        at = pl.ds(pl.multiple_of(place, 8), lay.wide)
        for part in range(2):
            results[step][part, : lay.wide] = whole[part, at, :]


def rows_from(lay, pieces, y_inverse, index):
    low, high = None, None
    for step, (real, imag) in enumerate(pieces):
        piece_slice = index ^ step
        sign = (1 - 2 * (piece_slice // (lay.slices // 2))).astype(F32)
        part = along_y(real, imag, y_inverse, piece_slice, True)
        turned = [value * sign for value in part]
        low = part if low is None else [a + b for a, b in zip(low, part)]
        high = turned if high is None else [a + b for a, b in zip(high, turned)]
    return low, high


def middle_kernel(lay, *refs):
    pieces = refs[: lay.slices]
    lens, injected, y_inverse, y_forward = refs[lay.slices : lay.slices + 4]
    own, other = refs[lay.slices + 4 : lay.slices + 6]
    results = refs[lay.slices + 6 : 2 * lay.slices + 6]
    fields, parity_parts = refs[-2:]
    index, side = lay.place()
    last = lax.axis_index("depth") == lay.groups - 1
    both = 2 * lay.rows
    low, high = rows_from(
        lay,
        [[piece[:, part].reshape(both, lay.cols) for part in range(2)] for piece in pieces],
        y_inverse,
        index,
    )
    for end, (real, imag) in enumerate((low, high)):
        lanes = pl.ds(end * lay.half, lay.half)
        cosine = lens[0, :, :, lanes].reshape(both, lay.half)
        sine = lens[1, :, :, lanes].reshape(both, lay.half)
        shape = (2, lay.rows, lay.half)
        fields[:, 0, :, lanes] = (real * cosine - imag * sine).reshape(shape)
        fields[:, 1, :, lanes] = (real * sine + imag * cosine).reshape(shape)
    for part in range(2):
        own[part] = fields[side, part]
        other[part] = fields[1 - side, part]
    for part in range(2):
        ends = []
        for end in range(2):
            lanes = pl.ds(end * lay.half, lay.half)
            value = jnp.where(last, injected[part, :, :, lanes], fields[:, part, :, lanes])
            ends.append(value.reshape(both, lay.half))
        parity_parts[0, part] = ends[0] + ends[1]
        parity_parts[1, part] = ends[0] - ends[1]
    for step in range(lay.slices):
        piece_slice = index ^ step
        at = piece_slice // (lay.slices // 2)
        pair = along_y(parity_parts[at, 0], parity_parts[at, 1], y_forward, piece_slice, False)
        for part in range(2):
            results[step][:, part] = pair[part].reshape(2, lay.rows, lay.cols)


def last_kernel(lay, *refs):
    pieces = refs[: lay.ranks]
    slow, scalars, inner, outer, y_inverse, previous = refs[lay.ranks : lay.ranks + 6]
    image_top, image_bottom, wave_out, image = refs[lay.ranks + 6 : lay.ranks + 10]
    lens, fields, wave_buffer, image_buffer, wave_sent, image_sent = refs[-6:]
    index, side = lay.place()
    freq = pieces[0][0, lay.wide : lay.wide + 1, 0:1]
    end = HALF + lay.rows
    before, behind = beside(inner, outer, 4)
    for start, values in ((0, before), (HALF, slow[...]), (end, behind)):
        sine, cosine = sin_cos(freq * (values - scalars[1:2, 0:1]) * DZ)
        lens[0, start : start + values.shape[0]] = cosine
        lens[1, start : start + values.shape[0]] = sine
    for turn in range(2):
        field = side ^ turn
        sign = (1 - 2 * field).astype(F32)
        ends = rows_from(
            lay,
            [
                [piece[part, : lay.wide] for part in range(2)]
                for piece in pieces[turn * lay.slices : (turn + 1) * lay.slices]
            ],
            y_inverse,
            index,
        )
        for end, (real, imag) in enumerate(ends):
            lanes = pl.ds(end * lay.half, lay.half)
            cosine, sine = lens[0, :, lanes], lens[1, :, lanes] * sign
            fields[field, 0, :, lanes] = real * cosine - imag * sine
            fields[field, 1, :, lanes] = real * sine + imag * cosine
    for field in range(2):
        for part in range(2):
            for chunk in range(lay.chunks):
                start = (part * lay.rows * 2 + field) * lay.chunks + chunk
                wave_buffer[pl.ds(start, lay.rows, stride=2 * lay.chunks), :] = fields[
                    field, part, HALF : HALF + lay.rows, pl.ds(chunk * LANES, LANES)
                ]
    copies = [pltpu.make_async_copy(wave_buffer, wave_out, wave_sent)]
    copies[0].start()
    stop = lay.rows - HALF
    for offset in range(OFF):
        value = correlation(fields, offset, lay.rows)
        image_buffer[offset, :HALF] = image_top[offset] + value[:HALF]
        image_buffer[offset, HALF:stop] = previous[offset, HALF:stop] + value[HALF:stop]
        image_buffer[offset, stop:] = image_bottom[offset] + value[stop:]
        copies.append(
            pltpu.make_async_copy(
                image_buffer.at[offset], image.at[offset], image_sent.at[offset]
            )
        )
        copies[-1].start()
    for copy in copies:
        copy.wait()


def correlation(fields, offset, rows):
    lag = offset - HALF
    source = pl.ds(HALF - lag, rows)
    receiver = pl.ds(HALF + lag, rows)
    return (
        fields[0, 0, source] * fields[1, 0, receiver]
        + fields[0, 1, source] * fields[1, 1, receiver]
    )


def beside(inner, outer, plane):
    is_odd = lax.axis_index("row") % 2 == 1
    one, two = inner[plane], outer[plane]
    return jnp.where(is_odd, one, two), jnp.where(is_odd, two, one)


def ends_kernel(lay, own, other, inner, outer, image_top, image_bottom, top, bottom):
    rank = lax.axis_index("row")
    side = rank // lay.slices
    side_before = (rank + lay.ranks - 1) % lay.ranks // lay.slices
    side_behind = (rank + 1) % lay.ranks // lay.slices
    start = lay.rows - 2 * HALF
    for part in range(2):
        for field, block in ((side, own), (1 - side, other)):
            top[field, part, HALF:] = block[part, : 2 * HALF]
            bottom[field, part, : 2 * HALF] = block[part, start:]
        for field in range(2):
            before, _ = beside(inner, outer, 2 * (field ^ side_before) + part)
            _, behind = beside(inner, outer, 2 * (field ^ side_behind) + part)
            top[field, part, :HALF] = before
            bottom[field, part, 2 * HALF :] = behind
    for offset in range(OFF):
        image_top[offset] = correlation(top, offset, HALF)
        image_bottom[offset] = correlation(bottom, offset, HALF)


def image_kernel(lay, own, other, slow, result, inner, outer, fields):
    _, side = lay.place()
    end = HALF + lay.rows
    nothing = jnp.zeros((2, HALF, lay.lateral), F32)
    for field, block in ((side, own), (1 - side, other)):
        fields[field, :, :HALF] = nothing
        fields[field, :, HALF:end] = block[...]
        fields[field, :, end:] = nothing
    for offset in range(OFF):
        result[offset] = correlation(fields, offset, lay.rows)
    is_odd = lax.axis_index("row") % 2 == 1
    planes = [own.at[0], own.at[1], other.at[0], other.at[1], slow]
    for at, plane in enumerate(planes):
        first, last = plane[:HALF], plane[lay.rows - HALF :]
        inner[at] = jnp.where(is_odd, first, last)
        outer[at] = jnp.where(is_odd, last, first)


def fill_phase(lay, wave_number, phase):
    index, side = lay.place()
    shape = (lay.half, lay.cols)
    spacing = 2.0 * math.pi / lay.lateral

    def squares(even_odd):
        signed = jnp.where(even_odd < lay.half, even_odd, even_odd - lay.lateral)
        number = signed.astype(F32) * spacing
        return number * number

    place = lax.broadcasted_iota(jnp.int32, (1, lay.cols), 1) + index * lay.cols
    y_squares = squares(jnp.where(place < lay.half, 2 * place, 2 * (place - lay.half) + 1))
    scale = 1.0 / (lay.lateral * lay.lateral)
    sign = (1 - 2 * side).astype(F32) * scale
    for parity in range(2):
        x_squares = squares(2 * lax.broadcasted_iota(jnp.int32, shape, 0) + parity)
        vertical = wave_number * wave_number - (x_squares + y_squares)
        argument = jnp.sqrt(jnp.abs(vertical)) * DZ
        sine, cosine = sin_cos(argument)
        runs = vertical > 0
        phase[0, parity] = jnp.where(runs, cosine, jnp.exp(-argument)) * scale
        phase[1, parity] = jnp.where(runs, sine, 0.0) * sign


def phase_kernel(lay, scalars, phase):
    fill_phase(lay, scalars[0:1, 0:1] * scalars[1:2, 0:1], phase)


def next_phase_kernel(lay, scalars, scalars_next, phase, freq_rows):
    last = lax.axis_index("depth") == lay.groups - 1
    freq_now = jnp.where(last, scalars[2:3, 0:1], scalars[0:1, 0:1])
    fill_phase(lay, freq_now * scalars_next[1:2, 0:1], phase)
    freq_rows[...] = jnp.zeros((8, lay.cols), F32) + freq_now


def inject_kernel(lay, *refs):
    far, injected = refs[:4], refs[4]
    sums, near, arrivals = refs[5], refs[6:10], refs[10]
    copies = [
        pltpu.make_async_copy(source, target, arrivals.at[i])
        for i, (source, target) in enumerate(zip(far, near))
    ]
    for copy in copies:
        copy.start()
    index, side = lay.place()
    source_at, wavelet, records, receivers = near
    count = receivers.shape[1]
    width = next((w for w in (1024, 512, 256, 128) if count % w == 0), count)
    both = 2 * lay.rows
    is_source = side == 0
    row = lax.broadcasted_iota(jnp.int32, (both, width), 0)
    row = row + index * lay.rows + jnp.where(row >= lay.rows, (lay.slices - 1) * lay.rows, 0)
    column = lax.broadcasted_iota(jnp.int32, (lay.lateral, width), 0)
    for copy in copies:
        copy.wait()
    for start in range(0, count, width):
        lanes = pl.ds(start, width)
        is_first = lax.broadcasted_iota(jnp.int32, (1, width), 1) + start == 0
        at_row = jnp.where(
            is_source, jnp.where(is_first, source_at[:, 0:1], -1), receivers[0:1, lanes]
        )
        at_column = jnp.where(is_source, source_at[:, 1:2], receivers[1:2, lanes])
        hit = row == at_row
        stacked = []
        for part in range(2):
            value = jnp.where(
                is_source, wavelet[:, part : part + 1], records[part : part + 1, lanes]
            )
            high = value.astype(BF16).astype(F32)
            for piece in (high, value - high):
                stacked.append(jnp.where(hit, piece, 0.0).astype(BF16))
        picked = jnp.where(column == at_column, 1.0, 0.0).astype(BF16)
        found = lax.dot_general(
            jnp.concatenate(stacked, axis=0),
            picked,
            (((1,), (1,)), ((), ())),
            preferred_element_type=F32,
        )
        sums[...] = found if start == 0 else sums[...] + found
    for part in range(2):
        at = 2 * part * both
        value = sums[at : at + both] + sums[at + both : at + 2 * both]
        injected[part] = value.reshape(2, lay.rows, lay.lateral)


def lens_kernel(lay, scalars, slow, *refs):
    lens = refs[-1]
    _, side = lay.place()
    sign = (1 - 2 * side).astype(F32)
    freq, ref_own = scalars[0:1, 0:1], scalars[1:2, 0:1]

    def store(field, start, values):
        sine, cosine = sin_cos(sign * freq * (values - ref_own) * DZ)
        at = pl.ds(pl.multiple_of(start, 8), values.shape[0])
        lens[0, field, at, :] = cosine
        lens[1, field, at, :] = sine

    store(side, 0, slow[...])
    shot = lax.axis_index("shots")
    for step, part in enumerate(refs[:-1]):
        start = (shot ^ step) * part.shape[0] if len(refs) > 2 else 0
        store(1 - side, start, part[...])


def after(*values):
    return lax.optimization_barrier(values)


def call(kernel, outs, scratch, args, far=(), outside=False, vmem=40, name=None):
    inside = pl.BlockSpec(memory_space=pltpu.VMEM)
    outer = pl.BlockSpec(memory_space=pltpu.HBM)
    anywhere = pl.BlockSpec(memory_space=pl.ANY)
    shapes = [jax.ShapeDtypeStruct(shape, F32) for shape in outs]
    args = [
        pltpu.with_memory_space_constraint(value, pltpu.HBM) if i in far else value
        for i, value in enumerate(args)
    ]
    return pl.pallas_call(
        kernel,
        out_shape=shapes,
        in_specs=[outer if i in far else inside for i in range(len(args))],
        out_specs=[anywhere if outside else inside] * len(outs),
        scratch_shapes=[
            pltpu.VMEM(shape, F32) if isinstance(shape, tuple) else shape for shape in scratch
        ],
        compiler_params=pltpu.CompilerParams(vmem_limit_bytes=vmem * MIB),
        cost_estimate=pl.CostEstimate(
            flops=1, bytes_accessed=1, transcendentals=0
        ),
        name=name,
    )(*args)


def local(waves, slab_freq, slowness, ref_slow, inj_freq, wavelet, records, src_pos, rcv_pos):
    ranks, groups = lax.axis_size("row"), lax.axis_size("depth")
    rows, lateral = waves.shape[2], waves.shape[5]
    lay = Layout(ranks, groups, rows, lateral)
    slices, cols, half = lay.slices, lay.cols, lay.half
    x_forward, x_inverse, y_forward, y_inverse = (
        jnp.asarray(table) for table in tables(lateral, slices)
    )
    slow = slowness[0]

    def exchange(value, step):
        return lax.ppermute(value, "row", [(rank, rank ^ step) for rank in range(ranks)])

    def onward(value, step):
        pairs = [
            (group * ranks + rank, (group + 1) % groups * ranks + (rank ^ step))
            for group in range(groups)
            for rank in range(ranks)
        ]
        return lax.ppermute(value, ("depth", "row"), pairs)

    piece = (2, rows, cols)
    pair_piece = (2, 2, rows, cols)
    block = (2, rows, lateral)
    wide = lay.wide
    flat = (2 * rows * 2 * lay.chunks, LANES)

    shots = lax.axis_size("shots")
    if shots & (shots - 1) or rows % (8 * shots):
        shots = 1
    share = rows // shots
    shot = lax.axis_index("shots") if shots > 1 else 0
    slow_parts = [exchange(lax.dynamic_slice_in_dim(slow, shot * share, share), slices)]

    phase = (2, 2, half, cols)
    column_scratch = [
        (2, 2, half, cols),
        (2, lateral + OFF, cols),
        pltpu.VMEM(x_inverse.shape, BF16),
        pltpu.SemaphoreType.DMA(()),
    ]
    sent = call(
        functools.partial(first_kernel, lay),
        [piece] * ranks,
        [
            (4, 2, rows, half),
            flat,
            pltpu.VMEM(y_forward.shape, BF16),
            pltpu.SemaphoreType.DMA((2,)),
        ],
        [waves.reshape(flat), y_forward],
        far=(0, 1),
        name="rows_to_columns",
    )
    sent, slow_parts = after(sent, slow_parts)
    arrived = [sent[0]] + [None] * (ranks - 1)
    for step in reversed(range(1, ranks)):
        arrived[step] = exchange(sent[step], step)
    for step in range(1, shots):
        pairs = [(shot, shot ^ step) for shot in range(shots)]
        slow_parts.append(lax.ppermute(slow_parts[0], "shots", pairs))

    values, _ = after((slab_freq[0, 0], ref_slow[0], inj_freq[0, 0]), sent[1])
    scalars = jnp.broadcast_to(
        jnp.pad(jnp.stack(values), (0, 5))[:, None], (8, LANES)
    )
    scalars_next = lax.ppermute(
        scalars, "depth", [(i, (i - 1) % groups) for i in range(groups)]
    )
    (phase_a,) = call(
        functools.partial(phase_kernel, lay),
        [phase],
        [],
        [scalars],
        name="phase_first",
    )
    receivers = [src_pos[None], wavelet[0], records.reshape(2, -1), rcv_pos.T]
    receivers[0], scalars_next = after(receivers[0], scalars_next)
    (injected,) = call(
        functools.partial(inject_kernel, lay),
        [(2, 2, rows, lateral)],
        [(8 * rows, lateral)]
        + [pltpu.VMEM(value.shape, value.dtype) for value in receivers]
        + [pltpu.SemaphoreType.DMA((4,))],
        receivers,
        far=(0, 1, 2, 3),
        name="injection",
    )
    phase_a, slow_parts, injected = after(phase_a, slow_parts, injected)
    sent = call(
        functools.partial(column_kernel, lay, True),
        [pair_piece] * slices,
        column_scratch,
        [*arrived, phase_a, x_forward, x_inverse],
        far=(ranks + 2,),
        name="columns_first",
    )
    scalars, scalars_next, sent = after(scalars, scalars_next, sent)
    arrived = [sent[0]] + [exchange(sent[step], step) for step in range(1, slices)]
    phase_b, freq_rows = call(
        functools.partial(next_phase_kernel, lay),
        [phase, (8, cols)],
        [],
        [scalars, scalars_next],
        name="phase_second",
    )
    (lens,) = call(
        functools.partial(lens_kernel, lay),
        [(2, 2, rows, lateral)],
        [],
        [scalars, slow, *slow_parts],
        name="lens",
    )
    lens, phase_b = after(lens, phase_b)
    own, other, *sent = call(
        functools.partial(middle_kernel, lay),
        [block, block] + [pair_piece] * slices,
        [(2, 2, rows, lateral), (2, 2, 2 * rows, half)],
        [*arrived, lens, injected, y_inverse, y_forward],
        name="columns_to_columns",
    )
    arrived = [sent[0]] + [exchange(sent[step], step) for step in range(1, slices)]
    other = exchange(other, slices)
    sent = call(
        functools.partial(column_kernel, lay, False),
        [(2, wide + 8, cols)] + [(2, wide, cols)] * (ranks - 1),
        column_scratch,
        [*arrived, phase_b, x_forward, x_inverse, freq_rows],
        far=(slices + 2,),
        name="columns_second",
    )
    arrived = [onward(value, step) for step, value in enumerate(sent)]

    previous, inner, outer = call(
        functools.partial(image_kernel, lay),
        [(OFF, rows, lateral)] + [(5, HALF, lateral)] * 2,
        [(2, 2, wide, lateral)],
        [own, other, slow],
        name="image_first",
    )
    inner = exchange(inner, 1)
    between = [(rank, rank + 1) for rank in range(1, ranks - 1, 2)]
    outer = lax.ppermute(
        outer, "row", between + [(target, source) for source, target in between]
    )
    image_top, image_bottom = call(
        functools.partial(ends_kernel, lay),
        [(OFF, HALF, lateral)] * 2,
        [(2, 2, 3 * HALF, lateral)] * 2,
        [own, other, inner, outer],
        name="image_ends",
    )
    wave_out, result = call(
        functools.partial(last_kernel, lay),
        [flat, (OFF, rows, lateral)],
        [
            (2, wide, lateral),
            (2, 2, wide, lateral),
            flat,
            (OFF, rows, lateral),
            pltpu.SemaphoreType.DMA(()),
            pltpu.SemaphoreType.DMA((OFF,)),
        ],
        [*arrived, slow, scalars, inner, outer, y_inverse, previous, image_top, image_bottom],
        outside=True,
        name="last_rows_and_image",
    )
    return wave_out.reshape(waves.shape), result[None]


def solution(mesh):
    placed = (
        P(("shots", "depth"), None, "row", None, None, None),
        P(("shots", "depth"), None),
        P("depth", "row", None),
        P("depth"),
        P("shots", None),
        P("shots", None, None),
        P("shots", None, None, None),
        P("shots"),
        P("shots", None),
    )
    return jax.shard_map(
        local,
        mesh=mesh,
        in_specs=placed,
        out_specs=(
            P(("shots", "depth"), None, "row", None, None, None),
            P(("shots", "depth"), None, "row", None),
        ),
        check_vma=False,
    )
```

```python
import functools
import math

import jax
import jax.numpy as jnp
import ml_dtypes
import numpy as np
from jax import lax
from jax.experimental import pallas as pl
from jax.experimental.pallas import tpu as pltpu
from jax.sharding import PartitionSpec as P

OFF = 16
HALF = OFF // 2
DZ = 4
LANES = 128
MIB = 1024 * 1024

F32 = jnp.float32
BF16 = jnp.bfloat16


def wave_order(length):
    place = np.arange(length)
    half = length // 2
    return np.where(place < half, 2 * place, 2 * (place - half) + 1)


def two_parts(table):
    high = table.astype(ml_dtypes.bfloat16)
    low = (table - high.astype(np.float64)).astype(ml_dtypes.bfloat16)
    return np.stack([high, low])


@functools.lru_cache(maxsize=None)
def tables(length, slices):
    half, cols = length // 2, length // slices
    product = wave_order(length)[:, None] * np.arange(half)[None, :] % length
    angle = product * (2.0 * math.pi / length)
    pair = np.stack([np.cos(angle), np.sin(angle)])
    by_parity = pair.reshape(2, 2, half, half)
    x_forward = by_parity.transpose(1, 0, 2, 3).reshape(2, 2 * half, half)
    x_inverse = by_parity.transpose(1, 0, 3, 2).reshape(2, 2 * half, half)
    y_inverse = pair.reshape(2, slices, cols, half)
    y_forward = y_inverse.transpose(0, 1, 3, 2)
    return tuple(two_parts(t) for t in (x_forward, x_inverse, y_forward, y_inverse))


def parts_of(value):
    high = value.astype(BF16)
    return high, (value - high.astype(F32)).astype(BF16)


def dot(a, b):
    return jnp.dot(a, b, preferred_element_type=F32)


def sin_cos(angle):
    turns = jnp.floor(angle * (2.0 / math.pi) + 0.5)
    rest = angle - turns * 1.5703125
    rest = rest - turns * 4.837512969970703125e-4
    rest = rest - turns * 7.54978995489188216e-8
    square = rest * rest
    sine = rest + rest * square * (
        -1.6666654611e-1 + square * (8.3321608736e-3 - square * 1.9515295891e-4)
    )
    cosine = 1.0 + square * (
        -0.5
        + square * (4.166664568298827e-2 + square * (-1.388731625493765e-3 + square * 2.443315711809948e-5))
    )
    quarter = turns.astype(jnp.int32)
    swap = (quarter & 1) == 1
    sine_out = jnp.where(swap, cosine, sine)
    cosine_out = jnp.where(swap, sine, cosine)
    sine_out = jnp.where((quarter & 2) == 2, -sine_out, sine_out)
    cosine_out = jnp.where(((quarter + 1) & 2) == 2, -cosine_out, cosine_out)
    return sine_out, cosine_out


def along_y(real, imag, table, index, inverse):
    rows = real.shape[0]
    real_high, real_low = parts_of(real)
    imag_high, imag_low = parts_of(imag)
    stacked = jnp.concatenate([real_high, imag_high, real_low, imag_low], axis=0)
    products = []
    for which in range(2):
        both = dot(stacked, table[0, which, index])
        products.append(
            both[: 2 * rows] + (both[2 * rows :] + dot(stacked[: 2 * rows], table[1, which, index]))
        )
    cosines, sines = products
    if inverse:
        return cosines[:rows] - sines[rows:], cosines[rows:] + sines[:rows]
    return cosines[:rows] + sines[rows:], cosines[rows:] - sines[:rows]


def along_x(real, imag, table, parity, inverse):
    half = real.shape[0]
    products = []
    for value in (real, imag):
        high, low = parts_of(value)
        products.append(
            dot(table[0, parity], high)
            + (dot(table[0, parity], low) + dot(table[1, parity], high))
        )
    by_real, by_imag = products
    if inverse:
        return by_real[:half] - by_imag[half:], by_imag[:half] + by_real[half:]
    return by_real[:half] + by_imag[half:], by_imag[:half] - by_real[half:]


class Layout:
    def __init__(self, ranks, groups, rows, lateral):
        self.ranks, self.groups, self.rows, self.lateral = ranks, groups, rows, lateral
        self.slices = ranks // 2
        self.half = lateral // 2
        self.cols = lateral // self.slices
        self.chunks = lateral // LANES
        self.wide = rows + OFF

    def place(self):
        rank = lax.axis_index("row")
        return rank % self.slices, rank // self.slices


def first_kernel(lay, *refs):
    far, pieces = refs[:2], refs[2 : 2 + lay.ranks]
    parity_parts, waves, y_forward, arrivals = refs[2 + lay.ranks :]
    index, side = lay.place()
    middle = lay.chunks // 2
    copies = [
        pltpu.make_async_copy(source, target, arrivals.at[i])
        for i, (source, target) in enumerate(zip(far, (waves, y_forward)))
    ]
    for copy in copies:
        copy.start()
    copies[0].wait()
    for field in range(2):
        for part in range(2):
            chunks = [
                waves[
                    pl.ds(
                        (part * lay.rows * 2 + field) * lay.chunks + chunk,
                        lay.rows,
                        stride=2 * lay.chunks,
                    ),
                    :,
                ]
                for chunk in range(lay.chunks)
            ]
            low = jnp.concatenate(chunks[:middle], axis=1)
            high = jnp.concatenate(chunks[middle:], axis=1)
            parity_parts[2 * field, part] = low + high
            parity_parts[2 * field + 1, part] = low - high
    copies[1].wait()
    for step in reversed(range(lay.ranks)):
        piece_slice = index ^ (step % lay.slices)
        field = side ^ (step // lay.slices)
        at = 2 * field + piece_slice // (lay.slices // 2)
        real, imag = along_y(
            parity_parts[at, 0], parity_parts[at, 1], y_forward, piece_slice, False
        )
        pieces[step][0] = real
        pieces[step][1] = imag


def column_kernel(lay, first, *refs):
    count_in = lay.ranks if first else lay.slices
    count_out = lay.slices if first else lay.ranks
    pieces = refs[:count_in]
    phase, x_forward, x_inverse_far = refs[count_in : count_in + 3]
    results = refs[-4 - count_out : -4]
    parity_parts, whole, x_inverse, x_inverse_here = refs[-4:]
    x_inverse_copy = pltpu.make_async_copy(x_inverse_far, x_inverse, x_inverse_here)
    x_inverse_copy.start()
    index, side = lay.place()
    sign = (1 - 2 * side).astype(F32)
    for step in range(lay.slices):
        at = pl.ds(pl.multiple_of((index ^ step) * lay.rows, lay.rows), lay.rows)
        for part in range(2):
            if first:
                low, high = pieces[step][part], pieces[step + lay.slices][part]
                difference = (low - high) * sign
            else:
                low, high = pieces[step][0, part], pieces[step][1, part]
                difference = low - high
            parity_parts[0, part, at, :] = low + high
            parity_parts[1, part, at, :] = difference
    shifted = []
    for parity in range(2):
        real, imag = along_x(
            parity_parts[parity, 0], parity_parts[parity, 1], x_forward, parity, False
        )
        phase_real, phase_imag = phase[0, parity], phase[1, parity]
        shifted.append(
            (real * phase_real - imag * phase_imag, real * phase_imag + imag * phase_real)
        )
    x_inverse_copy.wait()
    sums = [along_x(*shifted[parity], x_inverse, parity, True) for parity in range(2)]
    for part in range(2):
        whole[part, :HALF] = jnp.zeros((HALF, lay.cols), F32)
        whole[part, HALF : HALF + lay.half] = sums[0][part] + sums[1][part]
        whole[part, HALF + lay.half : HALF + lay.lateral] = sums[0][part] - sums[1][part]
        whole[part, HALF + lay.lateral :] = jnp.zeros((HALF, lay.cols), F32)
    if first:
        for step in range(lay.slices):
            for upper in range(2):
                place = ((index ^ step) + upper * lay.slices) * lay.rows
                at = pl.ds(pl.multiple_of(place + HALF, 8), lay.rows)
                for part in range(2):
                    results[step][upper, part] = whole[part, at, :]
        return
    results[0][0, lay.wide :] = refs[count_in + 3][...]
    for step in range(lay.ranks):
        place = ((index + side * lay.slices) ^ step) * lay.rows
        at = pl.ds(pl.multiple_of(place, 8), lay.wide)
        for part in range(2):
            results[step][part, : lay.wide] = whole[part, at, :]


def rows_from(lay, pieces, y_inverse, index):
    low, high = None, None
    for step, (real, imag) in enumerate(pieces):
        piece_slice = index ^ step
        sign = (1 - 2 * (piece_slice // (lay.slices // 2))).astype(F32)
        part = along_y(real, imag, y_inverse, piece_slice, True)
        turned = [value * sign for value in part]
        low = part if low is None else [a + b for a, b in zip(low, part)]
        high = turned if high is None else [a + b for a, b in zip(high, turned)]
    return low, high


def middle_kernel(lay, *refs):
    pieces = refs[: lay.slices]
    lens, injected, y_inverse, y_forward = refs[lay.slices : lay.slices + 4]
    own, other = refs[lay.slices + 4 : lay.slices + 6]
    results = refs[lay.slices + 6 : 2 * lay.slices + 6]
    fields, parity_parts = refs[-2:]
    index, side = lay.place()
    last = lax.axis_index("depth") == lay.groups - 1
    both = 2 * lay.rows
    low, high = rows_from(
        lay,
        [[piece[:, part].reshape(both, lay.cols) for part in range(2)] for piece in pieces],
        y_inverse,
        index,
    )
    for end, (real, imag) in enumerate((low, high)):
        lanes = pl.ds(end * lay.half, lay.half)
        cosine = lens[0, :, :, lanes].reshape(both, lay.half)
        sine = lens[1, :, :, lanes].reshape(both, lay.half)
        shape = (2, lay.rows, lay.half)
        fields[:, 0, :, lanes] = (real * cosine - imag * sine).reshape(shape)
        fields[:, 1, :, lanes] = (real * sine + imag * cosine).reshape(shape)
    for part in range(2):
        own[part] = fields[side, part]
        other[part] = fields[1 - side, part]
    for part in range(2):
        ends = []
        for end in range(2):
            lanes = pl.ds(end * lay.half, lay.half)
            value = jnp.where(last, injected[part, :, :, lanes], fields[:, part, :, lanes])
            ends.append(value.reshape(both, lay.half))
        parity_parts[0, part] = ends[0] + ends[1]
        parity_parts[1, part] = ends[0] - ends[1]
    for step in range(lay.slices):
        piece_slice = index ^ step
        at = piece_slice // (lay.slices // 2)
        pair = along_y(parity_parts[at, 0], parity_parts[at, 1], y_forward, piece_slice, False)
        for part in range(2):
            results[step][:, part] = pair[part].reshape(2, lay.rows, lay.cols)


def rows_of_pieces(lay, pieces, y_inverse):
    index, _ = lay.place()
    return rows_from(
        lay,
        [[piece[part, : lay.wide] for part in range(2)] for piece in pieces],
        y_inverse,
        index,
    )


def own_rows_kernel(lay, *refs):
    pieces, y_inverse, own = refs[: lay.slices], refs[lay.slices], refs[-1]
    for end, pair in enumerate(rows_of_pieces(lay, pieces, y_inverse)):
        for part in range(2):
            own[part, :, pl.ds(end * lay.half, lay.half)] = pair[part]


def last_kernel(lay, *refs):
    near, own, pieces = refs[0], refs[1], refs[2 : 2 + lay.slices]
    slow, scalars, inner, outer, y_inverse, previous = refs[2 + lay.slices : 8 + lay.slices]
    image_top, image_bottom, wave_out, image = refs[8 + lay.slices : 12 + lay.slices]
    lens, fields, wave_buffer, image_buffer, wave_sent, image_sent = refs[-6:]
    index, side = lay.place()
    freq = near[0, lay.wide : lay.wide + 1, 0:1]
    end = HALF + lay.rows
    before, behind = beside(inner, outer, 4)
    for start, values in ((0, before), (HALF, slow[...]), (end, behind)):
        sine, cosine = sin_cos(freq * (values - scalars[1:2, 0:1]) * DZ)
        lens[0, start : start + values.shape[0]] = cosine
        lens[1, start : start + values.shape[0]] = sine
    for turn in range(2):
        field = side ^ turn
        sign = (1 - 2 * field).astype(F32)
        if turn == 0:
            ends = [
                [own[part, :, pl.ds(end * lay.half, lay.half)] for part in range(2)]
                for end in range(2)
            ]
        else:
            ends = rows_of_pieces(lay, pieces, y_inverse)
        for end, (real, imag) in enumerate(ends):
            lanes = pl.ds(end * lay.half, lay.half)
            cosine, sine = lens[0, :, lanes], lens[1, :, lanes] * sign
            fields[field, 0, :, lanes] = real * cosine - imag * sine
            fields[field, 1, :, lanes] = real * sine + imag * cosine
    for field in range(2):
        for part in range(2):
            for chunk in range(lay.chunks):
                start = (part * lay.rows * 2 + field) * lay.chunks + chunk
                wave_buffer[pl.ds(start, lay.rows, stride=2 * lay.chunks), :] = fields[
                    field, part, HALF : HALF + lay.rows, pl.ds(chunk * LANES, LANES)
                ]
    copies = [pltpu.make_async_copy(wave_buffer, wave_out, wave_sent)]
    copies[0].start()
    stop = lay.rows - HALF
    for offset in range(OFF):
        value = correlation(fields, offset, lay.rows)
        image_buffer[offset, :HALF] = image_top[offset] + value[:HALF]
        image_buffer[offset, HALF:stop] = previous[offset, HALF:stop] + value[HALF:stop]
        image_buffer[offset, stop:] = image_bottom[offset] + value[stop:]
        copies.append(
            pltpu.make_async_copy(
                image_buffer.at[offset], image.at[offset], image_sent.at[offset]
            )
        )
        copies[-1].start()
    for copy in copies:
        copy.wait()


def correlation(fields, offset, rows):
    lag = offset - HALF
    source = pl.ds(HALF - lag, rows)
    receiver = pl.ds(HALF + lag, rows)
    return (
        fields[0, 0, source] * fields[1, 0, receiver]
        + fields[0, 1, source] * fields[1, 1, receiver]
    )


def beside(inner, outer, plane):
    is_odd = lax.axis_index("row") % 2 == 1
    one, two = inner[plane], outer[plane]
    return jnp.where(is_odd, one, two), jnp.where(is_odd, two, one)


def ends_kernel(lay, own, other, inner, outer, image_top, image_bottom, top, bottom):
    rank = lax.axis_index("row")
    side = rank // lay.slices
    side_before = (rank + lay.ranks - 1) % lay.ranks // lay.slices
    side_behind = (rank + 1) % lay.ranks // lay.slices
    start = lay.rows - 2 * HALF
    for part in range(2):
        for field, block in ((side, own), (1 - side, other)):
            top[field, part, HALF:] = block[part, : 2 * HALF]
            bottom[field, part, : 2 * HALF] = block[part, start:]
        for field in range(2):
            before, _ = beside(inner, outer, 2 * (field ^ side_before) + part)
            _, behind = beside(inner, outer, 2 * (field ^ side_behind) + part)
            top[field, part, :HALF] = before
            bottom[field, part, 2 * HALF :] = behind
    for offset in range(OFF):
        image_top[offset] = correlation(top, offset, HALF)
        image_bottom[offset] = correlation(bottom, offset, HALF)


def image_kernel(lay, own, other, slow, result, inner, outer, fields):
    _, side = lay.place()
    end = HALF + lay.rows
    nothing = jnp.zeros((2, HALF, lay.lateral), F32)
    for field, block in ((side, own), (1 - side, other)):
        fields[field, :, :HALF] = nothing
        fields[field, :, HALF:end] = block[...]
        fields[field, :, end:] = nothing
    for offset in range(OFF):
        result[offset] = correlation(fields, offset, lay.rows)
    is_odd = lax.axis_index("row") % 2 == 1
    planes = [own.at[0], own.at[1], other.at[0], other.at[1], slow]
    for at, plane in enumerate(planes):
        first, last = plane[:HALF], plane[lay.rows - HALF :]
        inner[at] = jnp.where(is_odd, first, last)
        outer[at] = jnp.where(is_odd, last, first)


def fill_phase(lay, wave_number, phase):
    index, side = lay.place()
    shape = (lay.half, lay.cols)
    spacing = 2.0 * math.pi / lay.lateral

    def squares(even_odd):
        signed = jnp.where(even_odd < lay.half, even_odd, even_odd - lay.lateral)
        number = signed.astype(F32) * spacing
        return number * number

    place = lax.broadcasted_iota(jnp.int32, (1, lay.cols), 1) + index * lay.cols
    y_squares = squares(jnp.where(place < lay.half, 2 * place, 2 * (place - lay.half) + 1))
    scale = 1.0 / (lay.lateral * lay.lateral)
    sign = (1 - 2 * side).astype(F32) * scale
    for parity in range(2):
        x_squares = squares(2 * lax.broadcasted_iota(jnp.int32, shape, 0) + parity)
        vertical = wave_number * wave_number - (x_squares + y_squares)
        argument = jnp.sqrt(jnp.abs(vertical)) * DZ
        sine, cosine = sin_cos(argument)
        runs = vertical > 0
        phase[0, parity] = jnp.where(runs, cosine, jnp.exp(-argument)) * scale
        phase[1, parity] = jnp.where(runs, sine, 0.0) * sign


def phase_kernel(lay, scalars, phase):
    fill_phase(lay, scalars[0:1, 0:1] * scalars[1:2, 0:1], phase)


def next_phase_kernel(lay, scalars, scalars_next, phase, freq_rows):
    last = lax.axis_index("depth") == lay.groups - 1
    freq_now = jnp.where(last, scalars[2:3, 0:1], scalars[0:1, 0:1])
    fill_phase(lay, freq_now * scalars_next[1:2, 0:1], phase)
    freq_rows[...] = jnp.zeros((8, lay.cols), F32) + freq_now


def inject_kernel(lay, *refs):
    far, injected = refs[:4], refs[4]
    sums, near, arrivals = refs[5], refs[6:10], refs[10]
    copies = [
        pltpu.make_async_copy(source, target, arrivals.at[i])
        for i, (source, target) in enumerate(zip(far, near))
    ]
    for copy in copies:
        copy.start()
    index, side = lay.place()
    source_at, wavelet, records, receivers = near
    count = receivers.shape[1]
    width = next((w for w in (1024, 512, 256, 128) if count % w == 0), count)
    both = 2 * lay.rows
    is_source = side == 0
    row = lax.broadcasted_iota(jnp.int32, (both, width), 0)
    row = row + index * lay.rows + jnp.where(row >= lay.rows, (lay.slices - 1) * lay.rows, 0)
    column = lax.broadcasted_iota(jnp.int32, (lay.lateral, width), 0)
    for copy in copies:
        copy.wait()
    for start in range(0, count, width):
        lanes = pl.ds(start, width)
        is_first = lax.broadcasted_iota(jnp.int32, (1, width), 1) + start == 0
        at_row = jnp.where(
            is_source, jnp.where(is_first, source_at[:, 0:1], -1), receivers[0:1, lanes]
        )
        at_column = jnp.where(is_source, source_at[:, 1:2], receivers[1:2, lanes])
        hit = row == at_row
        stacked = []
        for part in range(2):
            value = jnp.where(
                is_source, wavelet[:, part : part + 1], records[part : part + 1, lanes]
            )
            high = value.astype(BF16).astype(F32)
            for piece in (high, value - high):
                stacked.append(jnp.where(hit, piece, 0.0).astype(BF16))
        picked = jnp.where(column == at_column, 1.0, 0.0).astype(BF16)
        found = lax.dot_general(
            jnp.concatenate(stacked, axis=0),
            picked,
            (((1,), (1,)), ((), ())),
            preferred_element_type=F32,
        )
        sums[...] = found if start == 0 else sums[...] + found
    for part in range(2):
        at = 2 * part * both
        value = sums[at : at + both] + sums[at + both : at + 2 * both]
        injected[part] = value.reshape(2, lay.rows, lay.lateral)


def lens_kernel(lay, scalars, slow, *refs):
    lens = refs[-1]
    _, side = lay.place()
    sign = (1 - 2 * side).astype(F32)
    freq, ref_own = scalars[0:1, 0:1], scalars[1:2, 0:1]

    def store(field, start, values):
        sine, cosine = sin_cos(sign * freq * (values - ref_own) * DZ)
        at = pl.ds(pl.multiple_of(start, 8), values.shape[0])
        lens[0, field, at, :] = cosine
        lens[1, field, at, :] = sine

    store(side, 0, slow[...])
    shot = lax.axis_index("shots")
    for step, part in enumerate(refs[:-1]):
        start = (shot ^ step) * part.shape[0] if len(refs) > 2 else 0
        store(1 - side, start, part[...])


def after(*values):
    return lax.optimization_barrier(values)


def call(kernel, outs, scratch, args, far=(), outside=False, vmem=40, name=None):
    inside = pl.BlockSpec(memory_space=pltpu.VMEM)
    outer = pl.BlockSpec(memory_space=pltpu.HBM)
    anywhere = pl.BlockSpec(memory_space=pl.ANY)
    shapes = [jax.ShapeDtypeStruct(shape, F32) for shape in outs]
    args = [
        pltpu.with_memory_space_constraint(value, pltpu.HBM) if i in far else value
        for i, value in enumerate(args)
    ]
    return pl.pallas_call(
        kernel,
        out_shape=shapes,
        in_specs=[outer if i in far else inside for i in range(len(args))],
        out_specs=[anywhere if outside else inside] * len(outs),
        scratch_shapes=[
            pltpu.VMEM(shape, F32) if isinstance(shape, tuple) else shape for shape in scratch
        ],
        compiler_params=pltpu.CompilerParams(vmem_limit_bytes=vmem * MIB),
        cost_estimate=pl.CostEstimate(
            flops=1, bytes_accessed=1, transcendentals=0
        ),
        name=name,
    )(*args)


def local(waves, slab_freq, slowness, ref_slow, inj_freq, wavelet, records, src_pos, rcv_pos):
    ranks, groups = lax.axis_size("row"), lax.axis_size("depth")
    rows, lateral = waves.shape[2], waves.shape[5]
    lay = Layout(ranks, groups, rows, lateral)
    slices, cols, half = lay.slices, lay.cols, lay.half
    x_forward, x_inverse, y_forward, y_inverse = (
        jnp.asarray(table) for table in tables(lateral, slices)
    )
    slow = slowness[0]

    def exchange(value, step):
        return lax.ppermute(value, "row", [(rank, rank ^ step) for rank in range(ranks)])

    def onward(value, step):
        pairs = [
            (group * ranks + rank, (group + 1) % groups * ranks + (rank ^ step))
            for group in range(groups)
            for rank in range(ranks)
        ]
        return lax.ppermute(value, ("depth", "row"), pairs)

    piece = (2, rows, cols)
    pair_piece = (2, 2, rows, cols)
    block = (2, rows, lateral)
    wide = lay.wide
    flat = (2 * rows * 2 * lay.chunks, LANES)

    shots = lax.axis_size("shots")
    if shots & (shots - 1) or rows % (8 * shots):
        shots = 1
    share = rows // shots
    shot = lax.axis_index("shots") if shots > 1 else 0
    slow_parts = [exchange(lax.dynamic_slice_in_dim(slow, shot * share, share), slices)]

    phase = (2, 2, half, cols)
    column_scratch = [
        (2, 2, half, cols),
        (2, lateral + OFF, cols),
        pltpu.VMEM(x_inverse.shape, BF16),
        pltpu.SemaphoreType.DMA(()),
    ]
    sent = call(
        functools.partial(first_kernel, lay),
        [piece] * ranks,
        [
            (4, 2, rows, half),
            flat,
            pltpu.VMEM(y_forward.shape, BF16),
            pltpu.SemaphoreType.DMA((2,)),
        ],
        [waves.reshape(flat), y_forward],
        far=(0, 1),
        name="rows_to_columns",
    )
    sent, slow_parts = after(sent, slow_parts)
    arrived = [sent[0]] + [None] * (ranks - 1)
    for step in reversed(range(1, ranks)):
        arrived[step] = exchange(sent[step], step)
    for step in range(1, shots):
        pairs = [(shot, shot ^ step) for shot in range(shots)]
        slow_parts.append(lax.ppermute(slow_parts[0], "shots", pairs))

    values, _ = after((slab_freq[0, 0], ref_slow[0], inj_freq[0, 0]), sent[1])
    scalars = jnp.broadcast_to(
        jnp.pad(jnp.stack(values), (0, 5))[:, None], (8, LANES)
    )
    scalars_next = lax.ppermute(
        scalars, "depth", [(i, (i - 1) % groups) for i in range(groups)]
    )
    (phase_a,) = call(
        functools.partial(phase_kernel, lay),
        [phase],
        [],
        [scalars],
        name="phase_first",
    )
    receivers = [src_pos[None], wavelet[0], records.reshape(2, -1), rcv_pos.T]
    receivers[0], scalars_next = after(receivers[0], scalars_next)
    (injected,) = call(
        functools.partial(inject_kernel, lay),
        [(2, 2, rows, lateral)],
        [(8 * rows, lateral)]
        + [pltpu.VMEM(value.shape, value.dtype) for value in receivers]
        + [pltpu.SemaphoreType.DMA((4,))],
        receivers,
        far=(0, 1, 2, 3),
        name="injection",
    )
    phase_a, slow_parts, injected = after(phase_a, slow_parts, injected)
    sent = call(
        functools.partial(column_kernel, lay, True),
        [pair_piece] * slices,
        column_scratch,
        [*arrived, phase_a, x_forward, x_inverse],
        far=(ranks + 2,),
        name="columns_first",
    )
    scalars, scalars_next, sent = after(scalars, scalars_next, sent)
    arrived = [sent[0]] + [exchange(sent[step], step) for step in range(1, slices)]
    phase_b, freq_rows = call(
        functools.partial(next_phase_kernel, lay),
        [phase, (8, cols)],
        [],
        [scalars, scalars_next],
        name="phase_second",
    )
    (lens,) = call(
        functools.partial(lens_kernel, lay),
        [(2, 2, rows, lateral)],
        [],
        [scalars, slow, *slow_parts],
        name="lens",
    )
    lens, phase_b = after(lens, phase_b)
    own, other, *sent = call(
        functools.partial(middle_kernel, lay),
        [block, block] + [pair_piece] * slices,
        [(2, 2, rows, lateral), (2, 2, 2 * rows, half)],
        [*arrived, lens, injected, y_inverse, y_forward],
        name="columns_to_columns",
    )
    arrived = [sent[0]] + [exchange(sent[step], step) for step in range(1, slices)]
    other = exchange(other, slices)
    sent = call(
        functools.partial(column_kernel, lay, False),
        [(2, wide + 8, cols)] + [(2, wide, cols)] * (ranks - 1),
        column_scratch,
        [*arrived, phase_b, x_forward, x_inverse, freq_rows],
        far=(slices + 2,),
        name="columns_second",
    )
    arrived = [onward(value, step) for step, value in enumerate(sent)]

    (own_rows,) = call(
        functools.partial(own_rows_kernel, lay),
        [(2, wide, lateral)],
        [],
        [*arrived[:slices], y_inverse],
        name="own_rows",
    )

    previous, inner, outer = call(
        functools.partial(image_kernel, lay),
        [(OFF, rows, lateral)] + [(5, HALF, lateral)] * 2,
        [(2, 2, wide, lateral)],
        [own, other, slow],
        name="image_first",
    )
    inner = exchange(inner, 1)
    outer, own_rows = after(outer, own_rows)
    between = [(rank, rank + 1) for rank in range(1, ranks - 1, 2)]
    outer = lax.ppermute(
        outer, "row", between + [(target, source) for source, target in between]
    )
    image_top, image_bottom = call(
        functools.partial(ends_kernel, lay),
        [(OFF, HALF, lateral)] * 2,
        [(2, 2, 3 * HALF, lateral)] * 2,
        [own, other, inner, outer],
        name="image_ends",
    )
    wave_out, result = call(
        functools.partial(last_kernel, lay),
        [flat, (OFF, rows, lateral)],
        [
            (2, wide, lateral),
            (2, 2, wide, lateral),
            flat,
            (OFF, rows, lateral),
            pltpu.SemaphoreType.DMA(()),
            pltpu.SemaphoreType.DMA((OFF,)),
        ],
        [arrived[0], own_rows, *arrived[slices:], slow, scalars, inner, outer, y_inverse, previous, image_top, image_bottom],
        outside=True,
        name="last_rows_and_image",
    )
    return wave_out.reshape(waves.shape), result[None]


def solution(mesh):
    placed = (
        P(("shots", "depth"), None, "row", None, None, None),
        P(("shots", "depth"), None),
        P("depth", "row", None),
        P("depth"),
        P("shots", None),
        P("shots", None, None),
        P("shots", None, None, None),
        P("shots"),
        P("shots", None),
    )
    return jax.shard_map(
        local,
        mesh=mesh,
        in_specs=placed,
        out_specs=(
            P(("shots", "depth"), None, "row", None, None, None),
            P(("shots", "depth"), None, "row", None),
        ),
        check_vma=False,
    )
```

```python
import functools
import math

import jax
import jax.numpy as jnp
import ml_dtypes
import numpy as np
from jax import lax
from jax.experimental import pallas as pl
from jax.experimental.pallas import tpu as pltpu
from jax.sharding import PartitionSpec as P

OFF = 16
HALF = OFF // 2
DZ = 4
LANES = 128
MIB = 1024 * 1024

F32 = jnp.float32
BF16 = jnp.bfloat16


def wave_order(length):
    place = np.arange(length)
    half = length // 2
    return np.where(place < half, 2 * place, 2 * (place - half) + 1)


def two_parts(table):
    high = table.astype(ml_dtypes.bfloat16)
    low = (table - high.astype(np.float64)).astype(ml_dtypes.bfloat16)
    return np.stack([high, low])


@functools.lru_cache(maxsize=None)
def tables(length, slices):
    half, cols = length // 2, length // slices
    product = wave_order(length)[:, None] * np.arange(half)[None, :] % length
    angle = product * (2.0 * math.pi / length)
    pair = np.stack([np.cos(angle), np.sin(angle)])
    by_parity = pair.reshape(2, 2, half, half)
    x_forward = by_parity.transpose(1, 0, 2, 3).reshape(2, 2 * half, half)
    x_inverse = by_parity.transpose(1, 0, 3, 2).reshape(2, 2 * half, half)
    y_inverse = pair.reshape(2, slices, cols, half)
    y_forward = y_inverse.transpose(0, 1, 3, 2)
    return tuple(two_parts(t) for t in (x_forward, x_inverse, y_forward, y_inverse))


def parts_of(value):
    high = value.astype(BF16)
    return high, (value - high.astype(F32)).astype(BF16)


def dot(a, b):
    return jnp.dot(a, b, preferred_element_type=F32)


def sin_cos(angle):
    turns = jnp.floor(angle * (2.0 / math.pi) + 0.5)
    rest = angle - turns * 1.5703125
    rest = rest - turns * 4.837512969970703125e-4
    rest = rest - turns * 7.54978995489188216e-8
    square = rest * rest
    sine = rest + rest * square * (
        -1.6666654611e-1 + square * (8.3321608736e-3 - square * 1.9515295891e-4)
    )
    cosine = 1.0 + square * (
        -0.5
        + square * (4.166664568298827e-2 + square * (-1.388731625493765e-3 + square * 2.443315711809948e-5))
    )
    quarter = turns.astype(jnp.int32)
    swap = (quarter & 1) == 1
    sine_out = jnp.where(swap, cosine, sine)
    cosine_out = jnp.where(swap, sine, cosine)
    sine_out = jnp.where((quarter & 2) == 2, -sine_out, sine_out)
    cosine_out = jnp.where(((quarter + 1) & 2) == 2, -cosine_out, cosine_out)
    return sine_out, cosine_out


def along_y(real, imag, table, index, inverse):
    rows = real.shape[0]
    real_high, real_low = parts_of(real)
    imag_high, imag_low = parts_of(imag)
    stacked = jnp.concatenate([real_high, imag_high, real_low, imag_low], axis=0)
    products = []
    for which in range(2):
        both = dot(stacked, table[0, which, index])
        products.append(
            both[: 2 * rows] + (both[2 * rows :] + dot(stacked[: 2 * rows], table[1, which, index]))
        )
    cosines, sines = products
    if inverse:
        return cosines[:rows] - sines[rows:], cosines[rows:] + sines[:rows]
    return cosines[:rows] + sines[rows:], cosines[rows:] - sines[:rows]


def along_x(real, imag, table, parity, inverse):
    half = real.shape[0]
    products = []
    for value in (real, imag):
        high, low = parts_of(value)
        products.append(
            dot(table[0, parity], high)
            + (dot(table[0, parity], low) + dot(table[1, parity], high))
        )
    by_real, by_imag = products
    if inverse:
        return by_real[:half] - by_imag[half:], by_imag[:half] + by_real[half:]
    return by_real[:half] + by_imag[half:], by_imag[:half] - by_real[half:]


class Layout:
    def __init__(self, ranks, groups, rows, lateral):
        self.ranks, self.groups, self.rows, self.lateral = ranks, groups, rows, lateral
        self.slices = ranks // 2
        self.half = lateral // 2
        self.cols = lateral // self.slices
        self.chunks = lateral // LANES
        self.wide = rows + OFF

    def place(self):
        rank = lax.axis_index("row")
        return rank % self.slices, rank // self.slices


def first_kernel(lay, *refs):
    far, pieces = refs[:2], refs[2 : 2 + lay.ranks]
    parity_parts, waves, y_forward, arrivals = refs[2 + lay.ranks :]
    index, side = lay.place()
    middle = lay.chunks // 2
    copies = [
        pltpu.make_async_copy(source, target, arrivals.at[i])
        for i, (source, target) in enumerate(zip(far, (waves, y_forward)))
    ]
    for copy in copies:
        copy.start()
    copies[0].wait()
    for field in range(2):
        for part in range(2):
            chunks = [
                waves[
                    pl.ds(
                        (part * lay.rows * 2 + field) * lay.chunks + chunk,
                        lay.rows,
                        stride=2 * lay.chunks,
                    ),
                    :,
                ]
                for chunk in range(lay.chunks)
            ]
            low = jnp.concatenate(chunks[:middle], axis=1)
            high = jnp.concatenate(chunks[middle:], axis=1)
            parity_parts[2 * field, part] = low + high
            parity_parts[2 * field + 1, part] = low - high
    copies[1].wait()
    for step in reversed(range(lay.ranks)):
        piece_slice = index ^ (step % lay.slices)
        field = side ^ (step // lay.slices)
        at = 2 * field + piece_slice // (lay.slices // 2)
        real, imag = along_y(
            parity_parts[at, 0], parity_parts[at, 1], y_forward, piece_slice, False
        )
        pieces[step][0] = real
        pieces[step][1] = imag


def column_kernel(lay, first, *refs):
    count_in = lay.ranks if first else lay.slices
    count_out = lay.slices if first else lay.ranks
    pieces = refs[:count_in]
    phase, x_forward, x_inverse_far = refs[count_in : count_in + 3]
    results = refs[-4 - count_out : -4]
    parity_parts, whole, x_inverse, x_inverse_here = refs[-4:]
    x_inverse_copy = pltpu.make_async_copy(x_inverse_far, x_inverse, x_inverse_here)
    x_inverse_copy.start()
    index, side = lay.place()
    sign = (1 - 2 * side).astype(F32)
    for step in range(lay.slices):
        at = pl.ds(pl.multiple_of((index ^ step) * lay.rows, lay.rows), lay.rows)
        for part in range(2):
            if first:
                low, high = pieces[step][part], pieces[step + lay.slices][part]
                difference = (low - high) * sign
            else:
                low, high = pieces[step][0, part], pieces[step][1, part]
                difference = low - high
            parity_parts[0, part, at, :] = low + high
            parity_parts[1, part, at, :] = difference
    shifted = []
    for parity in range(2):
        real, imag = along_x(
            parity_parts[parity, 0], parity_parts[parity, 1], x_forward, parity, False
        )
        phase_real, phase_imag = phase[0, parity], phase[1, parity]
        shifted.append(
            (real * phase_real - imag * phase_imag, real * phase_imag + imag * phase_real)
        )
    x_inverse_copy.wait()
    sums = [along_x(*shifted[parity], x_inverse, parity, True) for parity in range(2)]
    for part in range(2):
        whole[part, :HALF] = jnp.zeros((HALF, lay.cols), F32)
        whole[part, HALF : HALF + lay.half] = sums[0][part] + sums[1][part]
        whole[part, HALF + lay.half : HALF + lay.lateral] = sums[0][part] - sums[1][part]
        whole[part, HALF + lay.lateral :] = jnp.zeros((HALF, lay.cols), F32)
    if first:
        for step in range(lay.slices):
            for upper in range(2):
                place = ((index ^ step) + upper * lay.slices) * lay.rows
                at = pl.ds(pl.multiple_of(place + HALF, 8), lay.rows)
                for part in range(2):
                    results[step][upper, part] = whole[part, at, :]
        return
    results[0][0, lay.wide :] = refs[count_in + 3][...]
    for step in range(lay.ranks):
        place = ((index + side * lay.slices) ^ step) * lay.rows
        at = pl.ds(pl.multiple_of(place, 8), lay.wide)
        for part in range(2):
            results[step][part, : lay.wide] = whole[part, at, :]


def rows_from(lay, pieces, y_inverse, index):
    low, high = None, None
    for step, (real, imag) in enumerate(pieces):
        piece_slice = index ^ step
        sign = (1 - 2 * (piece_slice // (lay.slices // 2))).astype(F32)
        part = along_y(real, imag, y_inverse, piece_slice, True)
        turned = [value * sign for value in part]
        low = part if low is None else [a + b for a, b in zip(low, part)]
        high = turned if high is None else [a + b for a, b in zip(high, turned)]
    return low, high


def middle_kernel(lay, *refs):
    pieces = refs[: lay.slices]
    lens, injected, y_inverse, y_forward = refs[lay.slices : lay.slices + 4]
    own, other = refs[lay.slices + 4 : lay.slices + 6]
    results = refs[lay.slices + 6 : 2 * lay.slices + 6]
    fields, parity_parts = refs[-2:]
    index, side = lay.place()
    last = lax.axis_index("depth") == lay.groups - 1
    both = 2 * lay.rows
    low, high = rows_from(
        lay,
        [[piece[:, part].reshape(both, lay.cols) for part in range(2)] for piece in pieces],
        y_inverse,
        index,
    )
    for end, (real, imag) in enumerate((low, high)):
        lanes = pl.ds(end * lay.half, lay.half)
        cosine = lens[0, :, :, lanes].reshape(both, lay.half)
        sine = lens[1, :, :, lanes].reshape(both, lay.half)
        shape = (2, lay.rows, lay.half)
        fields[:, 0, :, lanes] = (real * cosine - imag * sine).reshape(shape)
        fields[:, 1, :, lanes] = (real * sine + imag * cosine).reshape(shape)
    for part in range(2):
        own[part] = fields[side, part]
        other[part] = fields[1 - side, part]
    for part in range(2):
        ends = []
        for end in range(2):
            lanes = pl.ds(end * lay.half, lay.half)
            value = jnp.where(last, injected[part, :, :, lanes], fields[:, part, :, lanes])
            ends.append(value.reshape(both, lay.half))
        parity_parts[0, part] = ends[0] + ends[1]
        parity_parts[1, part] = ends[0] - ends[1]
    for step in range(lay.slices):
        piece_slice = index ^ step
        at = piece_slice // (lay.slices // 2)
        pair = along_y(parity_parts[at, 0], parity_parts[at, 1], y_forward, piece_slice, False)
        for part in range(2):
            results[step][:, part] = pair[part].reshape(2, lay.rows, lay.cols)


def last_kernel(lay, *refs):
    pieces = refs[: lay.ranks]
    slow, scalars, inner, outer, y_inverse, previous = refs[lay.ranks : lay.ranks + 6]
    image_top, image_bottom, wave_out, image = refs[lay.ranks + 6 : lay.ranks + 10]
    lens, fields, wave_buffer, image_buffer, wave_sent, image_sent = refs[-6:]
    index, side = lay.place()
    freq = pieces[0][0, lay.wide : lay.wide + 1, 0:1]
    end = HALF + lay.rows
    before, behind = beside(inner, outer, 4)
    for start, values in ((0, before), (HALF, slow[...]), (end, behind)):
        sine, cosine = sin_cos(freq * (values - scalars[1:2, 0:1]) * DZ)
        lens[0, start : start + values.shape[0]] = cosine
        lens[1, start : start + values.shape[0]] = sine
    for turn in range(2):
        field = side ^ turn
        sign = (1 - 2 * field).astype(F32)
        ends = rows_from(
            lay,
            [
                [piece[part, : lay.wide] for part in range(2)]
                for piece in pieces[turn * lay.slices : (turn + 1) * lay.slices]
            ],
            y_inverse,
            index,
        )
        for end, (real, imag) in enumerate(ends):
            lanes = pl.ds(end * lay.half, lay.half)
            cosine, sine = lens[0, :, lanes], lens[1, :, lanes] * sign
            fields[field, 0, :, lanes] = real * cosine - imag * sine
            fields[field, 1, :, lanes] = real * sine + imag * cosine
    copies = []
    stop = lay.rows - HALF
    for offset in range(OFF):
        value = correlation(fields, offset, lay.rows)
        image_buffer[offset, :HALF] = image_top[offset] + value[:HALF]
        image_buffer[offset, HALF:stop] = previous[offset, HALF:stop] + value[HALF:stop]
        image_buffer[offset, stop:] = image_bottom[offset] + value[stop:]
        copies.append(
            pltpu.make_async_copy(
                image_buffer.at[offset], image.at[offset], image_sent.at[offset]
            )
        )
        copies[-1].start()
        if offset == OFF // 2:
            for field in range(2):
                for part in range(2):
                    for chunk in range(lay.chunks):
                        start = (part * lay.rows * 2 + field) * lay.chunks + chunk
                        wave_buffer[pl.ds(start, lay.rows, stride=2 * lay.chunks), :] = fields[
                            field, part, HALF : HALF + lay.rows, pl.ds(chunk * LANES, LANES)
                        ]
            copies.append(pltpu.make_async_copy(wave_buffer, wave_out, wave_sent))
            copies[-1].start()
    for copy in copies:
        copy.wait()


def correlation(fields, offset, rows):
    lag = offset - HALF
    source = pl.ds(HALF - lag, rows)
    receiver = pl.ds(HALF + lag, rows)
    return (
        fields[0, 0, source] * fields[1, 0, receiver]
        + fields[0, 1, source] * fields[1, 1, receiver]
    )


def beside(inner, outer, plane):
    is_odd = lax.axis_index("row") % 2 == 1
    one, two = inner[plane], outer[plane]
    return jnp.where(is_odd, one, two), jnp.where(is_odd, two, one)


def ends_kernel(lay, own, other, inner, outer, image_top, image_bottom, top, bottom):
    rank = lax.axis_index("row")
    side = rank // lay.slices
    side_before = (rank + lay.ranks - 1) % lay.ranks // lay.slices
    side_behind = (rank + 1) % lay.ranks // lay.slices
    start = lay.rows - 2 * HALF
    for part in range(2):
        for field, block in ((side, own), (1 - side, other)):
            top[field, part, HALF:] = block[part, : 2 * HALF]
            bottom[field, part, : 2 * HALF] = block[part, start:]
        for field in range(2):
            before, _ = beside(inner, outer, 2 * (field ^ side_before) + part)
            _, behind = beside(inner, outer, 2 * (field ^ side_behind) + part)
            top[field, part, :HALF] = before
            bottom[field, part, 2 * HALF :] = behind
    for offset in range(OFF):
        image_top[offset] = correlation(top, offset, HALF)
        image_bottom[offset] = correlation(bottom, offset, HALF)


def image_kernel(lay, own, other, slow, result, inner, outer, fields):
    _, side = lay.place()
    end = HALF + lay.rows
    nothing = jnp.zeros((2, HALF, lay.lateral), F32)
    for field, block in ((side, own), (1 - side, other)):
        fields[field, :, :HALF] = nothing
        fields[field, :, HALF:end] = block[...]
        fields[field, :, end:] = nothing
    for offset in range(OFF):
        result[offset] = correlation(fields, offset, lay.rows)
    is_odd = lax.axis_index("row") % 2 == 1
    planes = [own.at[0], own.at[1], other.at[0], other.at[1], slow]
    for at, plane in enumerate(planes):
        first, last = plane[:HALF], plane[lay.rows - HALF :]
        inner[at] = jnp.where(is_odd, first, last)
        outer[at] = jnp.where(is_odd, last, first)


def fill_phase(lay, wave_number, phase):
    index, side = lay.place()
    shape = (lay.half, lay.cols)
    spacing = 2.0 * math.pi / lay.lateral

    def squares(even_odd):
        signed = jnp.where(even_odd < lay.half, even_odd, even_odd - lay.lateral)
        number = signed.astype(F32) * spacing
        return number * number

    place = lax.broadcasted_iota(jnp.int32, (1, lay.cols), 1) + index * lay.cols
    y_squares = squares(jnp.where(place < lay.half, 2 * place, 2 * (place - lay.half) + 1))
    scale = 1.0 / (lay.lateral * lay.lateral)
    sign = (1 - 2 * side).astype(F32) * scale
    for parity in range(2):
        x_squares = squares(2 * lax.broadcasted_iota(jnp.int32, shape, 0) + parity)
        vertical = wave_number * wave_number - (x_squares + y_squares)
        argument = jnp.sqrt(jnp.abs(vertical)) * DZ
        sine, cosine = sin_cos(argument)
        runs = vertical > 0
        phase[0, parity] = jnp.where(runs, cosine, jnp.exp(-argument)) * scale
        phase[1, parity] = jnp.where(runs, sine, 0.0) * sign


def phase_kernel(lay, scalars, phase):
    fill_phase(lay, scalars[0:1, 0:1] * scalars[1:2, 0:1], phase)


def next_phase_kernel(lay, scalars, scalars_next, phase, freq_rows):
    last = lax.axis_index("depth") == lay.groups - 1
    freq_now = jnp.where(last, scalars[2:3, 0:1], scalars[0:1, 0:1])
    fill_phase(lay, freq_now * scalars_next[1:2, 0:1], phase)
    freq_rows[...] = jnp.zeros((8, lay.cols), F32) + freq_now


def inject_kernel(lay, *refs):
    far, injected = refs[:4], refs[4]
    sums, near, arrivals = refs[5], refs[6:10], refs[10]
    copies = [
        pltpu.make_async_copy(source, target, arrivals.at[i])
        for i, (source, target) in enumerate(zip(far, near))
    ]
    for copy in copies:
        copy.start()
    index, side = lay.place()
    source_at, wavelet, records, receivers = near
    count = receivers.shape[1]
    width = next((w for w in (1024, 512, 256, 128) if count % w == 0), count)
    both = 2 * lay.rows
    is_source = side == 0
    row = lax.broadcasted_iota(jnp.int32, (both, width), 0)
    row = row + index * lay.rows + jnp.where(row >= lay.rows, (lay.slices - 1) * lay.rows, 0)
    column = lax.broadcasted_iota(jnp.int32, (lay.lateral, width), 0)
    for copy in copies:
        copy.wait()
    for start in range(0, count, width):
        lanes = pl.ds(start, width)
        is_first = lax.broadcasted_iota(jnp.int32, (1, width), 1) + start == 0
        at_row = jnp.where(
            is_source, jnp.where(is_first, source_at[:, 0:1], -1), receivers[0:1, lanes]
        )
        at_column = jnp.where(is_source, source_at[:, 1:2], receivers[1:2, lanes])
        hit = row == at_row
        stacked = []
        for part in range(2):
            value = jnp.where(
                is_source, wavelet[:, part : part + 1], records[part : part + 1, lanes]
            )
            high = value.astype(BF16).astype(F32)
            for piece in (high, value - high):
                stacked.append(jnp.where(hit, piece, 0.0).astype(BF16))
        picked = jnp.where(column == at_column, 1.0, 0.0).astype(BF16)
        found = lax.dot_general(
            jnp.concatenate(stacked, axis=0),
            picked,
            (((1,), (1,)), ((), ())),
            preferred_element_type=F32,
        )
        sums[...] = found if start == 0 else sums[...] + found
    for part in range(2):
        at = 2 * part * both
        value = sums[at : at + both] + sums[at + both : at + 2 * both]
        injected[part] = value.reshape(2, lay.rows, lay.lateral)


def lens_kernel(lay, scalars, slow, *refs):
    lens = refs[-1]
    _, side = lay.place()
    sign = (1 - 2 * side).astype(F32)
    freq, ref_own = scalars[0:1, 0:1], scalars[1:2, 0:1]

    def store(field, start, values):
        sine, cosine = sin_cos(sign * freq * (values - ref_own) * DZ)
        at = pl.ds(pl.multiple_of(start, 8), values.shape[0])
        lens[0, field, at, :] = cosine
        lens[1, field, at, :] = sine

    store(side, 0, slow[...])
    shot = lax.axis_index("shots")
    for step, part in enumerate(refs[:-1]):
        start = (shot ^ step) * part.shape[0] if len(refs) > 2 else 0
        store(1 - side, start, part[...])


def after(*values):
    return lax.optimization_barrier(values)


def call(kernel, outs, scratch, args, far=(), outside=False, vmem=40, name=None):
    inside = pl.BlockSpec(memory_space=pltpu.VMEM)
    outer = pl.BlockSpec(memory_space=pltpu.HBM)
    anywhere = pl.BlockSpec(memory_space=pl.ANY)
    shapes = [jax.ShapeDtypeStruct(shape, F32) for shape in outs]
    args = [
        pltpu.with_memory_space_constraint(value, pltpu.HBM) if i in far else value
        for i, value in enumerate(args)
    ]
    return pl.pallas_call(
        kernel,
        out_shape=shapes,
        in_specs=[outer if i in far else inside for i in range(len(args))],
        out_specs=[anywhere if outside else inside] * len(outs),
        scratch_shapes=[
            pltpu.VMEM(shape, F32) if isinstance(shape, tuple) else shape for shape in scratch
        ],
        compiler_params=pltpu.CompilerParams(vmem_limit_bytes=vmem * MIB),
        cost_estimate=pl.CostEstimate(
            flops=1, bytes_accessed=1, transcendentals=0
        ),
        name=name,
    )(*args)


def local(waves, slab_freq, slowness, ref_slow, inj_freq, wavelet, records, src_pos, rcv_pos):
    ranks, groups = lax.axis_size("row"), lax.axis_size("depth")
    rows, lateral = waves.shape[2], waves.shape[5]
    lay = Layout(ranks, groups, rows, lateral)
    slices, cols, half = lay.slices, lay.cols, lay.half
    x_forward, x_inverse, y_forward, y_inverse = (
        jnp.asarray(table) for table in tables(lateral, slices)
    )
    slow = slowness[0]

    def exchange(value, step):
        return lax.ppermute(value, "row", [(rank, rank ^ step) for rank in range(ranks)])

    def onward(value, step):
        pairs = [
            (group * ranks + rank, (group + 1) % groups * ranks + (rank ^ step))
            for group in range(groups)
            for rank in range(ranks)
        ]
        return lax.ppermute(value, ("depth", "row"), pairs)

    piece = (2, rows, cols)
    pair_piece = (2, 2, rows, cols)
    block = (2, rows, lateral)
    wide = lay.wide
    flat = (2 * rows * 2 * lay.chunks, LANES)

    shots = lax.axis_size("shots")
    if shots & (shots - 1) or rows % (8 * shots):
        shots = 1
    share = rows // shots
    shot = lax.axis_index("shots") if shots > 1 else 0
    slow_parts = [exchange(lax.dynamic_slice_in_dim(slow, shot * share, share), slices)]

    phase = (2, 2, half, cols)
    column_scratch = [
        (2, 2, half, cols),
        (2, lateral + OFF, cols),
        pltpu.VMEM(x_inverse.shape, BF16),
        pltpu.SemaphoreType.DMA(()),
    ]
    sent = call(
        functools.partial(first_kernel, lay),
        [piece] * ranks,
        [
            (4, 2, rows, half),
            flat,
            pltpu.VMEM(y_forward.shape, BF16),
            pltpu.SemaphoreType.DMA((2,)),
        ],
        [waves.reshape(flat), y_forward],
        far=(0, 1),
        name="rows_to_columns",
    )
    sent, slow_parts = after(sent, slow_parts)
    arrived = [sent[0]] + [None] * (ranks - 1)
    for step in reversed(range(1, ranks)):
        arrived[step] = exchange(sent[step], step)
    for step in range(1, shots):
        pairs = [(shot, shot ^ step) for shot in range(shots)]
        slow_parts.append(lax.ppermute(slow_parts[0], "shots", pairs))

    values, _ = after((slab_freq[0, 0], ref_slow[0], inj_freq[0, 0]), sent[1])
    scalars = jnp.broadcast_to(
        jnp.pad(jnp.stack(values), (0, 5))[:, None], (8, LANES)
    )
    scalars_next = lax.ppermute(
        scalars, "depth", [(i, (i - 1) % groups) for i in range(groups)]
    )
    (phase_a,) = call(
        functools.partial(phase_kernel, lay),
        [phase],
        [],
        [scalars],
        name="phase_first",
    )
    receivers = [src_pos[None], wavelet[0], records.reshape(2, -1), rcv_pos.T]
    receivers[0], scalars_next = after(receivers[0], scalars_next)
    (injected,) = call(
        functools.partial(inject_kernel, lay),
        [(2, 2, rows, lateral)],
        [(8 * rows, lateral)]
        + [pltpu.VMEM(value.shape, value.dtype) for value in receivers]
        + [pltpu.SemaphoreType.DMA((4,))],
        receivers,
        far=(0, 1, 2, 3),
        name="injection",
    )
    phase_a, slow_parts, injected = after(phase_a, slow_parts, injected)
    sent = call(
        functools.partial(column_kernel, lay, True),
        [pair_piece] * slices,
        column_scratch,
        [*arrived, phase_a, x_forward, x_inverse],
        far=(ranks + 2,),
        name="columns_first",
    )
    scalars, scalars_next, sent = after(scalars, scalars_next, sent)
    arrived = [sent[0]] + [exchange(sent[step], step) for step in range(1, slices)]
    phase_b, freq_rows = call(
        functools.partial(next_phase_kernel, lay),
        [phase, (8, cols)],
        [],
        [scalars, scalars_next],
        name="phase_second",
    )
    (lens,) = call(
        functools.partial(lens_kernel, lay),
        [(2, 2, rows, lateral)],
        [],
        [scalars, slow, *slow_parts],
        name="lens",
    )
    lens, phase_b = after(lens, phase_b)
    own, other, *sent = call(
        functools.partial(middle_kernel, lay),
        [block, block] + [pair_piece] * slices,
        [(2, 2, rows, lateral), (2, 2, 2 * rows, half)],
        [*arrived, lens, injected, y_inverse, y_forward],
        name="columns_to_columns",
    )
    arrived = [sent[0]] + [exchange(sent[step], step) for step in range(1, slices)]
    other = exchange(other, slices)
    sent = call(
        functools.partial(column_kernel, lay, False),
        [(2, wide + 8, cols)] + [(2, wide, cols)] * (ranks - 1),
        column_scratch,
        [*arrived, phase_b, x_forward, x_inverse, freq_rows],
        far=(slices + 2,),
        name="columns_second",
    )
    arrived = [onward(value, step) for step, value in enumerate(sent)]

    previous, inner, outer = call(
        functools.partial(image_kernel, lay),
        [(OFF, rows, lateral)] + [(5, HALF, lateral)] * 2,
        [(2, 2, wide, lateral)],
        [own, other, slow],
        name="image_first",
    )
    inner = exchange(inner, 1)
    between = [(rank, rank + 1) for rank in range(1, ranks - 1, 2)]
    outer = lax.ppermute(
        outer, "row", between + [(target, source) for source, target in between]
    )
    image_top, image_bottom = call(
        functools.partial(ends_kernel, lay),
        [(OFF, HALF, lateral)] * 2,
        [(2, 2, 3 * HALF, lateral)] * 2,
        [own, other, inner, outer],
        name="image_ends",
    )
    wave_out, result = call(
        functools.partial(last_kernel, lay),
        [flat, (OFF, rows, lateral)],
        [
            (2, wide, lateral),
            (2, 2, wide, lateral),
            flat,
            (OFF, rows, lateral),
            pltpu.SemaphoreType.DMA(()),
            pltpu.SemaphoreType.DMA((OFF,)),
        ],
        [*arrived, slow, scalars, inner, outer, y_inverse, previous, image_top, image_bottom],
        outside=True,
        name="last_rows_and_image",
    )
    return wave_out.reshape(waves.shape), result[None]


def solution(mesh):
    placed = (
        P(("shots", "depth"), None, "row", None, None, None),
        P(("shots", "depth"), None),
        P("depth", "row", None),
        P("depth"),
        P("shots", None),
        P("shots", None, None),
        P("shots", None, None, None),
        P("shots"),
        P("shots", None),
    )
    return jax.shard_map(
        local,
        mesh=mesh,
        in_specs=placed,
        out_specs=(
            P(("shots", "depth"), None, "row", None, None, None),
            P(("shots", "depth"), None, "row", None),
        ),
        check_vma=False,
    )
```
